256 devices in a mesh: lat: 16 (over y, x_hi, core), lon: 16 (over x_lo, z).
Axes of the slice: x: 4 (x_hi: 2, x_lo: 2; x = x_hi * 2 + x_lo), y: 4, z: 8, core: 2. Of those that a mesh axis runs over, the one named last changes fastest.
Arguments:
- field: bfloat16 [256, 512, 512], P('lat', 'lon'), may hold values from -6 to 6
- filter_values: bfloat16 [4, 256, 4, 4], replicated, may hold values from -1.5 to 1.5
- block_lat: int32 [256, 4], replicated, may hold values from -2 to 2, as said below
- block_lon: int32 [256, 4], replicated, may hold values from -16 to 13, as said below
- mixing: bfloat16 [4, 512, 512], replicated, may hold values from -0.125 to 0.125
- cotangent: bfloat16 [256, 512, 512], P('lat', 'lon'), may hold values from -6 to 6
Outputs:
- output: bfloat16 [256, 512, 512], P('lat', 'lon')
- field_grad: bfloat16 [256, 512, 512], P('lat', 'lon')
- mixing_grad: float32 [4, 512, 512], P(None, 'lat')
The draws below stay inside these ranges and needn't reach their ends.
Inputs may be any that keep to these rules, and one draw needn't show every extreme that they name: Block b of output cycle i reads input cycle i + block_lat[i, b]; the latitude reach of a cycle grows toward the poles, and every cycle has blocks at both ends of its reach. Block b of output cycle i covers longitude offsets block_lon[i, b] to block_lon[i, b] + 3; the longitude reach of a cycle grows toward the poles, and every cycle has blocks at both ends of its reach.
All inputs are finite; a program needn't handle non-finite values.
Results may differ from the reference program's by a relative error of at most 0.0049.
Values may be sent and summed in bfloat16 or wider, within the bound.
No kernel may reach another device: no remote copies, remote signals or barrier semaphores. Data moves between devices by JAX's collectives and lax.ppermute only.
A program may use at most 128 MiB of HBM per device.

```python
import math
import jax
import jax.numpy as jnp
from jax import lax

C = 512
KB = 4
NB = 4
BW = 4
HL = 2
WL = 16
NLAT = 256
NLON = 512


def pole_gap():
    cycle_ids = jnp.arange(NLAT, dtype=jnp.int32)
    return (cycle_ids, jnp.minimum(cycle_ids, NLAT - 1 - cycle_ids))


def draw_block_lat(key, part):
    key = jax.random.fold_in(key, 11)
    cycle_ids, distance = pole_gap()
    lat_reach = jnp.minimum(HL, 1 + NLAT // 4 // (distance + 1))[:, None]
    value_key, turn_key = jax.random.split(key)
    offsets = jax.random.randint(value_key, (NLAT, NB), -lat_reach, lat_reach + 1)
    rotation = jax.random.randint(turn_key, (), 0, NB)
    slot_ids = jnp.arange(NB, dtype=jnp.int32)[None, :]
    low_slot = ((cycle_ids + rotation) % NB)[:, None]
    high_slot = ((cycle_ids + rotation + 1) % NB)[:, None]
    offsets = jnp.where(slot_ids == low_slot, -lat_reach, offsets)
    offsets = jnp.where(slot_ids == high_slot, lat_reach, offsets)
    return offsets.astype(jnp.int32)


def draw_block_lon(key, part):
    key = jax.random.fold_in(key, 23)
    cycle_ids, distance = pole_gap()
    lon_reach = jnp.minimum(WL, BW + 2 * WL // (distance + 1))[:, None]
    value_key, turn_key = jax.random.split(key)
    offsets = jax.random.randint(value_key, (NLAT, NB), -lon_reach, lon_reach - BW + 2)
    rotation = jax.random.randint(turn_key, (), 0, NB)
    slot_ids = jnp.arange(NB, dtype=jnp.int32)[None, :]
    low_slot = ((cycle_ids + rotation + 2) % NB)[:, None]
    high_slot = ((cycle_ids + rotation + 3) % NB)[:, None]
    offsets = jnp.where(slot_ids == low_slot, -lon_reach, offsets)
    offsets = jnp.where(slot_ids == high_slot, lon_reach - BW + 1, offsets)
    return offsets.astype(jnp.int32)


def raised(array, key, source, target, shards_of, factor):
    owner, partner = [(jnp.arange(array.shape[axis_at]) // (array.shape[axis_at] // shards_of)).reshape([-1 if axis == axis_at else 1 for axis in range(array.ndim)]) for axis_at in (source, target)]
    chosen = jax.random.permutation(key, shards_of)[partner]
    strong = (owner == chosen) | (owner == (partner + shards_of // 2) % shards_of)
    return jnp.where(strong, factor * array, array)


def block_levels(key, extent, shards, low, top_value):
    gain = 1.0
    for position, shards_of in shards:
        draws = jax.random.uniform(jax.random.fold_in(jax.random.fold_in(key, 6), position), (shards_of,), jnp.float32, low / len(shards), top_value / len(shards))
        gain = gain * jnp.repeat(jnp.exp(draws), extent[position] // shards_of).reshape((-1,) + (1,) * (len(extent) - 1 - position))
    return gain


def normal_values(key, dims, deviation, reach, cuts=(), held_as=jnp.bfloat16):
    gain = block_levels(key, dims, cuts, -0.22, 0.18) if cuts else 1.0
    values = jax.random.normal(key, dims, jnp.float32) * deviation * gain
    return jnp.minimum(jnp.maximum(values, -reach), reach).astype(held_as)


def gaussian_with(own_key, dims, scale, bound, shards, heavy, held_as=jnp.bfloat16):
    array = scale * jax.random.normal(own_key, dims, jnp.float32)
    if shards:
        array = array * block_levels(own_key, dims, shards, -0.22, 0.18)
    return jnp.clip(raised(array, jax.random.fold_in(own_key, 3), *heavy), -bound, bound).astype(held_as)


def setup_inputs(seed: int = 0) -> dict:
    keys = jax.random.split(jax.random.key(seed), 7)
    field = gaussian_with(keys[0], (NLAT, NLON, C), 1.0, 6.0, ((0, 16), (1, 16)), (0, 2, 16, 2.0))
    filter_values = normal_values(keys[1], (KB, NLAT, NB, BW), 0.25, 1.5)
    block_lat = draw_block_lat(jax.random.fold_in(keys[6], 71), 0)
    block_lon = draw_block_lon(jax.random.fold_in(keys[6], 71), 0)
    mixing = normal_values(keys[4], (KB, C, C), (KB * C) ** -0.5, 0.125)
    cotangent = normal_values(keys[5], (NLAT, NLON, C), 1.0, 6.0, ((0, 16), (1, 16)))
    return {"field": field, "filter_values": filter_values, "block_lat": block_lat, "block_lon": block_lon, "mixing": mixing, "cotangent": cotangent}


def rotate_row(row_values, offset):
    doubled = jnp.concatenate([row_values, row_values], axis=0)
    start_index = jnp.mod(offset, NLON).astype(jnp.int32)
    return lax.dynamic_slice_in_dim(doubled, start_index, NLON, 0)

def reference(field, filter_values, block_lat, block_lon, mixing, cotangent):
    padded = jnp.pad(field, ((HL, HL), (0, 0), (0, 0)))
    mixing_wide = mixing.astype(jnp.float32)

    def cycle_step(state_pair, cycle_index):
        grad_rows, weight_sum = state_pair
        lat_row = block_lat[cycle_index]
        lon_row = block_lon[cycle_index]
        weights_row = filter_values[:, cycle_index].astype(jnp.float32)
        gathered = []
        for block_index in range(NB):
            source = lax.dynamic_index_in_dim(padded, cycle_index + HL + lat_row[block_index], 0, keepdims=False)
            for offset in range(BW):
                gathered.append(rotate_row(source, lon_row[block_index] + offset))
        stacked = jnp.stack(gathered).reshape(NB, BW, NLON, C).astype(jnp.float32)
        filtered = jnp.einsum('kbw,bwjc->kjc', weights_row, stacked).astype(jnp.bfloat16)
        filtered_wide = filtered.astype(jnp.float32)
        out_row = jnp.einsum('kjc,kcd->jd', filtered_wide, mixing_wide).astype(jnp.bfloat16)
        cot_row = cotangent[cycle_index].astype(jnp.float32)
        back_row = jnp.einsum('jd,kcd->kjc', cot_row, mixing_wide).astype(jnp.bfloat16)
        weight_sum = weight_sum + jnp.einsum('kjc,jd->kcd', filtered_wide, cot_row)
        pieces = jnp.einsum('kbw,kjc->bwjc', weights_row, back_row.astype(jnp.float32))
        for block_index in range(NB):
            spread = jnp.zeros((NLON, C), jnp.float32)
            for offset in range(BW):
                spread = spread + rotate_row(pieces[block_index, offset], -(lon_row[block_index] + offset))
            target = cycle_index + HL + lat_row[block_index]
            previous = lax.dynamic_slice_in_dim(grad_rows, target, 1, 0)
            grad_rows = lax.dynamic_update_slice_in_dim(grad_rows, previous + spread[None], target, 0)
        return ((grad_rows, weight_sum), out_row)
    start_state = (jnp.zeros((NLAT + 2 * HL, NLON, C), jnp.float32), jnp.zeros((KB, C, C), jnp.float32))
    final_state, output = lax.scan(cycle_step, start_state, jnp.arange(NLAT, dtype=jnp.int32))
    grad_rows, weight_sum = final_state
    field_grad = grad_rows[HL:HL + NLAT].astype(jnp.bfloat16)
    mixing_grad = weight_sum * (1.0 / math.sqrt(NLAT * NLON))
    return (output, field_grad, mixing_grad)
```

```python
import math

import jax
import jax.numpy as jnp
from jax import lax
from jax.experimental import pallas as pl
from jax.experimental.pallas import tpu as pltpu
from jax.sharding import Mesh
from jax.sharding import PartitionSpec as P

HL = 2
WL = 16
BW = 4
SPAN = 2 * HL + 1
F32 = jnp.float32
BF16 = jnp.bfloat16
VMEM = pl.BlockSpec(memory_space=pltpu.VMEM)
SMEM = pl.BlockSpec(memory_space=pltpu.SMEM)
PARAMS = pltpu.CompilerParams(vmem_limit_bytes=48 * 1024 * 1024)


def picked(distance, weights, basis, taps):
    value = jnp.zeros(distance.shape, F32)
    for tap in range(taps):
        row = weights[basis * taps + tap : basis * taps + tap + 1, :]
        value = jnp.where(distance == tap, row, value)
    return value


def taps_kernel(first, bank, fwd_out, adj_out):
    rows, basis_rows, _ = fwd_out.shape
    blocks, lines, cycles = bank.shape
    taps = BW
    basis_count = (lines - 2) // taps
    cols = basis_rows // basis_count
    wide = cols + 2 * WL
    near = 128 // blocks

    def iota(shape, axis):
        return lax.broadcasted_iota(jnp.int32, shape, axis)

    cycle = iota((cycles, 128), 0) - first[0] + HL
    slot = iota((cycles, 128), 1)
    fwd_bank = jnp.zeros((lines, 128), F32)
    adj_banks = []
    for block in range(blocks):
        lines_here = bank[block]
        hot = (slot == cycle + block * near) & (cycle >= 0) & (cycle < near)
        fwd_bank += jnp.dot(lines_here, hot.astype(BF16), preferred_element_type=F32)
        hot = (slot == cycle) & (cycle < near)
        adj_banks.append(jnp.dot(lines_here, hot.astype(BF16), preferred_element_type=F32))
    fwd_bank = fwd_bank.astype(BF16)
    adj_banks = [adj_bank.astype(BF16) for adj_bank in adj_banks]
    fwd_wide = blocks * wide
    adj_wide = SPAN * wide
    fwd_slot = iota((128, fwd_wide), 0) - (iota((128, fwd_wide), 1) // wide) * near - HL
    adj_slot = iota((128, adj_wide), 0) - iota((128, adj_wide), 1) // wide
    fwd_base = iota((cols, fwd_wide), 1) % wide - iota((cols, fwd_wide), 0) - WL
    adj_base = iota((cols, adj_wide), 0) - iota((cols, adj_wide), 1) % wide + WL
    adj_turn = HL - iota((1, adj_wide), 1) // wide

    def one_row(row, carry):
        hot = (fwd_slot == row).astype(BF16)
        weights = jnp.dot(fwd_bank, hot, preferred_element_type=F32)
        shift = weights[lines - 2 : lines - 1, :].astype(jnp.int32)
        distance = fwd_base - shift
        for basis in range(basis_count):
            value = picked(distance, weights, basis, taps)
            fwd_out[row, basis * cols : (basis + 1) * cols, :] = value.astype(BF16)
        hot = (adj_slot == row).astype(BF16)
        totals = [None] * basis_count
        for block in range(blocks):
            weights = jnp.dot(adj_banks[block], hot, preferred_element_type=F32)
            shift = weights[lines - 2 : lines - 1, :].astype(jnp.int32)
            turn = weights[lines - 1 : lines, :].astype(jnp.int32)
            distance = jnp.where(turn == adj_turn, adj_base - shift, -1)
            for basis in range(basis_count):
                value = picked(distance, weights, basis, taps)
                totals[basis] = value if block == 0 else totals[basis] + value
        for basis in range(basis_count):
            adj_out[row, basis * cols : (basis + 1) * cols, :] = totals[basis].astype(BF16)
        return carry

    lax.fori_loop(0, rows, one_row, 0, unroll=2)


def assemble(extended, center, west, east, north, south):
    rows, cols, _ = center.shape
    extended[HL : HL + rows, 0:WL] = west[...]
    extended[HL : HL + rows, WL : WL + cols] = center[...]
    extended[HL : HL + rows, WL + cols :] = east[...]
    extended[0:HL] = north[...]
    extended[HL + rows :] = south[...]


def filter_kernel(first, lat, taps, center, west, east, north, south, cot, weight_out, filt_out, extended):
    rows, cols, channels = center.shape
    basis_count = filt_out.shape[0]
    blocks = lat.shape[0]
    assemble(extended, center, west, east, north, south)

    def one_row(row, carry):
        slabs = [extended[row + HL + lat[block, first[0] + row]] for block in range(blocks)]
        slab = jnp.concatenate(slabs, axis=0)
        filtered = jnp.dot(taps[row], slab, preferred_element_type=F32).astype(BF16)
        filt_out[:, row] = filtered.reshape(basis_count, cols, channels)
        return carry

    lax.fori_loop(0, rows, one_row, 0, unroll=4)
    cot_flat = cot[...].reshape(rows * cols, channels)
    shares = weight_out.shape[0]
    for basis in range(basis_count):
        filtered = filt_out[basis].reshape(rows * cols, channels)
        terms = lax.dot_general(
            filtered, cot_flat, (((0,), (0,)), ((), ())), preferred_element_type=F32
        )
        weight_out[:, basis] = terms.reshape(shares, channels // shares, channels).astype(
            weight_out.dtype
        )


def output_kernel(filt, mixing, out):
    basis_count, rows, cols, channels = filt.shape
    total = None
    for basis in range(basis_count):
        part = jnp.dot(
            filt[basis].reshape(rows * cols, channels), mixing[basis], preferred_element_type=F32
        )
        total = part if total is None else total + part
    out[...] = total.reshape(rows, cols, channels).astype(BF16)


def adjoint_kernel(taps, center, west, east, north, south, mixing, out, extended, spread):
    rows, cols, channels = center.shape
    basis_count = mixing.shape[0]
    assemble(extended, center, west, east, north, south)

    def one_row(row, carry):
        slab = extended[pl.ds(row, SPAN)].reshape(SPAN * (cols + 2 * WL), channels)
        pulled = jnp.dot(taps[row], slab, preferred_element_type=F32).astype(BF16)
        spread[:, row] = pulled.reshape(basis_count, cols, channels)
        return carry

    lax.fori_loop(0, rows, one_row, 0, unroll=4)
    total = None
    for basis in range(basis_count):
        part = lax.dot_general(
            spread[basis].reshape(rows * cols, channels),
            mixing[basis],
            (((1,), (1,)), ((), ())),
            preferred_element_type=F32,
        )
        total = part if total is None else total + part
    out[...] = total.reshape(rows, cols, channels).astype(BF16)


def ring(step, count):
    return [(i, (i + step) % count) for i in range(count)]


def halo(cells):
    rows, cols, _ = cells.shape
    lons = lax.axis_size("lon")
    lats = lax.axis_size("lat")
    west = lax.ppermute(cells[:, cols - WL :], "lon", ring(1, lons))
    east = lax.ppermute(cells[:, :WL], "lon", ring(-1, lons))
    tail = jnp.concatenate([a[rows - HL :] for a in (west, cells, east)], axis=1)
    head = jnp.concatenate([a[:HL] for a in (west, cells, east)], axis=1)
    north = lax.ppermute(tail, "lat", [(i, i + 1) for i in range(lats - 1)])
    south = lax.ppermute(head, "lat", [(i + 1, i) for i in range(lats - 1)])
    return west, east, north, south


def local(field, filter_values, block_lat, block_lon, mixing, cotangent):
    rows, cols, channels = field.shape
    basis_count, _, blocks, taps = filter_values.shape
    first = (lax.axis_index("lat") * rows).astype(jnp.int32).reshape(1)
    field_halo = halo(field)
    cot_halo = halo(cotangent)

    psi_lines = filter_values.transpose(2, 0, 3, 1).reshape(blocks, basis_count * taps, -1)
    lat_lines = block_lat.T
    lon_lines = block_lon.T
    bank = jnp.concatenate(
        [psi_lines, lon_lines[:, None].astype(BF16), lat_lines[:, None].astype(BF16)], axis=1
    )
    wide = cols + 2 * WL
    fwd_taps, adj_taps = pl.pallas_call(
        taps_kernel,
        out_shape=(
            jax.ShapeDtypeStruct((rows, basis_count * cols, blocks * wide), BF16),
            jax.ShapeDtypeStruct((rows, basis_count * cols, SPAN * wide), BF16),
        ),
        in_specs=[SMEM, VMEM],
        out_specs=(VMEM, VMEM),
        compiler_params=PARAMS,
        name="taps",
    )(first, bank)

    lat_count = lax.axis_size("lat")
    share = channels // lat_count
    terms, filtered = pl.pallas_call(
        filter_kernel,
        out_shape=(
            jax.ShapeDtypeStruct((lat_count, basis_count, share, channels), BF16),
            jax.ShapeDtypeStruct((basis_count, rows, cols, channels), BF16),
        ),
        in_specs=[SMEM] * 2 + [VMEM] * 7,
        out_specs=(VMEM, VMEM),
        scratch_shapes=[pltpu.VMEM((rows + 2 * HL, wide, channels), BF16)],
        compiler_params=PARAMS,
        name="filtering",
    )(first, lat_lines, fwd_taps, field, *field_halo, cotangent)

    output = pl.pallas_call(
        output_kernel,
        out_shape=jax.ShapeDtypeStruct((rows, cols, channels), BF16),
        in_specs=[VMEM] * 2,
        out_specs=VMEM,
        compiler_params=PARAMS,
        name="mixed",
    )(filtered, mixing)

    field_grad = pl.pallas_call(
        adjoint_kernel,
        out_shape=jax.ShapeDtypeStruct((rows, cols, channels), BF16),
        in_specs=[VMEM] * 7,
        out_specs=VMEM,
        scratch_shapes=[
            pltpu.VMEM((rows + 2 * HL, wide, channels), BF16),
            pltpu.VMEM((basis_count, rows, cols, channels), BF16),
        ],
        compiler_params=PARAMS,
        name="adjoint",
    )(adj_taps, cotangent, *cot_halo, mixing)

    normalizer = 1.0 / math.sqrt(rows * lat_count * cols * lax.axis_size("lon"))
    summed = reduced(terms)
    return (output, field_grad, summed * normalizer)


def reduced(terms):
    summed = lax.psum_scatter(terms.astype(F32), "lat", scatter_dimension=0, tiled=True)
    return lax.psum(summed[0], "lon")


def solution(mesh):
    return jax.shard_map(
        local,
        mesh=mesh,
        in_specs=(P("lat", "lon", None), P(), P(), P(), P(), P("lat", "lon", None)),
        out_specs=(P("lat", "lon", None), P("lat", "lon", None), P(None, "lat", None)),
        check_vma=False,
    )
```

```python
import functools
import math

import jax
import jax.numpy as jnp
from jax import lax
from jax.experimental import pallas as pl
from jax.experimental.pallas import tpu as pltpu
from jax.sharding import Mesh
from jax.sharding import PartitionSpec as P

HL = 2
WL = 16
BW = 4
SPAN = 2 * HL + 1
F32 = jnp.float32
BF16 = jnp.bfloat16
VMEM = pl.BlockSpec(memory_space=pltpu.VMEM)
SMEM = pl.BlockSpec(memory_space=pltpu.SMEM)
PARAMS = pltpu.CompilerParams(vmem_limit_bytes=48 * 1024 * 1024)


def picked(distance, weights, basis, taps):
    value = jnp.zeros(distance.shape, F32)
    for tap in range(taps):
        row = weights[basis * taps + tap : basis * taps + tap + 1, :]
        value = jnp.where(distance == tap, row, value)
    return value


def taps_kernel(first, bank, fwd_out, adj_out):
    rows, basis_rows, _ = fwd_out.shape
    blocks, lines, cycles = bank.shape
    taps = BW
    basis_count = (lines - 2) // taps
    cols = basis_rows // basis_count
    wide = cols + 2 * WL
    near = 128 // blocks

    def iota(shape, axis):
        return lax.broadcasted_iota(jnp.int32, shape, axis)

    cycle = iota((cycles, 128), 0) - first[0] + HL
    slot = iota((cycles, 128), 1)
    fwd_bank = jnp.zeros((lines, 128), F32)
    adj_banks = []
    for block in range(blocks):
        lines_here = bank[block]
        hot = (slot == cycle + block * near) & (cycle >= 0) & (cycle < near)
        fwd_bank += jnp.dot(lines_here, hot.astype(BF16), preferred_element_type=F32)
        hot = (slot == cycle) & (cycle < near)
        adj_banks.append(jnp.dot(lines_here, hot.astype(BF16), preferred_element_type=F32))
    fwd_bank = fwd_bank.astype(BF16)
    adj_banks = [adj_bank.astype(BF16) for adj_bank in adj_banks]
    fwd_wide = blocks * wide
    adj_wide = SPAN * wide
    fwd_slot = iota((128, fwd_wide), 0) - (iota((128, fwd_wide), 1) // wide) * near - HL
    adj_slot = iota((128, adj_wide), 0) - iota((128, adj_wide), 1) // wide
    fwd_base = iota((cols, fwd_wide), 1) % wide - iota((cols, fwd_wide), 0) - WL
    adj_base = iota((cols, adj_wide), 0) - iota((cols, adj_wide), 1) % wide + WL
    adj_turn = HL - iota((1, adj_wide), 1) // wide

    def one_row(row, carry):
        hot = (fwd_slot == row).astype(BF16)
        weights = jnp.dot(fwd_bank, hot, preferred_element_type=F32)
        shift = weights[lines - 2 : lines - 1, :].astype(jnp.int32)
        distance = fwd_base - shift
        for basis in range(basis_count):
            value = picked(distance, weights, basis, taps)
            fwd_out[row, basis * cols : (basis + 1) * cols, :] = value.astype(BF16)
        hot = (adj_slot == row).astype(BF16)
        totals = [None] * basis_count
        for block in range(blocks):
            weights = jnp.dot(adj_banks[block], hot, preferred_element_type=F32)
            shift = weights[lines - 2 : lines - 1, :].astype(jnp.int32)
            turn = weights[lines - 1 : lines, :].astype(jnp.int32)
            distance = jnp.where(turn == adj_turn, adj_base - shift, -1)
            for basis in range(basis_count):
                value = picked(distance, weights, basis, taps)
                totals[basis] = value if block == 0 else totals[basis] + value
        for basis in range(basis_count):
            adj_out[row, basis * cols : (basis + 1) * cols, :] = totals[basis].astype(BF16)
        return carry

    lax.fori_loop(0, rows, one_row, 0, unroll=2)


def assemble(extended, center, west, east, north, south, rims_w, rims_e):
    rows, cols, _ = center.shape
    extended[HL : HL + rows, 0:WL] = west[...]
    extended[HL : HL + rows, WL : WL + cols] = center[...]
    extended[HL : HL + rows, WL + cols :] = east[...]
    extended[0:HL, WL : WL + cols] = north[...]
    extended[HL + rows :, WL : WL + cols] = south[...]
    extended[0:HL, 0:WL] = rims_w[0:HL]
    extended[HL + rows :, 0:WL] = rims_w[HL:]
    extended[0:HL, WL + cols :] = rims_e[0:HL]
    extended[HL + rows :, WL + cols :] = rims_e[HL:]


def filter_kernel(
    place, lat, taps, center, west, east, north, south, rims_w, rims_e, cot, keep, send, filt_out, extended
):
    rows, cols, channels = center.shape
    basis_count = filt_out.shape[0]
    blocks = lat.shape[0]
    assemble(extended, center, west, east, north, south, rims_w, rims_e)

    def one_row(row, carry):
        slabs = [extended[row + HL + lat[block, place[0] + row]] for block in range(blocks)]
        slab = jnp.concatenate(slabs, axis=0)
        filtered = jnp.dot(taps[row], slab, preferred_element_type=F32).astype(BF16)
        filt_out[:, row] = filtered.reshape(basis_count, cols, channels)
        return carry

    lax.fori_loop(0, rows, one_row, 0, unroll=4)
    cot_flat = cot[...].reshape(rows * cols, channels)
    pairs = keep.shape[0]
    share = channels // (2 * pairs)
    core = place[3]
    for basis in range(basis_count):
        filtered = filt_out[basis].reshape(rows * cols, channels)
        terms = lax.dot_general(
            filtered, cot_flat, (((0,), (0,)), ((), ())), preferred_element_type=F32
        ).reshape(pairs, 2, share, channels)
        lines = slice(basis * share, (basis + 1) * share)
        keep[:, lines] = jnp.where(core == 0, terms[:, 0], terms[:, 1])
        send[:, lines] = jnp.where(core == 0, terms[:, 1], terms[:, 0]).astype(BF16)


def output_kernel(filt, mixing, out):
    basis_count, rows, cols, channels = filt.shape
    total = None
    for basis in range(basis_count):
        part = jnp.dot(
            filt[basis].reshape(rows * cols, channels), mixing[basis], preferred_element_type=F32
        )
        total = part if total is None else total + part
    out[...] = total.reshape(rows, cols, channels).astype(BF16)


def adjoint_kernel(
    taps, center, west, east, north, south, rims_w, rims_e, mixing, out, extended, spread
):
    rows, cols, channels = center.shape
    basis_count = mixing.shape[0]
    assemble(extended, center, west, east, north, south, rims_w, rims_e)

    def one_row(row, carry):
        slab = extended[pl.ds(row, SPAN)].reshape(SPAN * (cols + 2 * WL), channels)
        pulled = jnp.dot(taps[row], slab, preferred_element_type=F32).astype(BF16)
        spread[:, row] = pulled.reshape(basis_count, cols, channels)
        return carry

    lax.fori_loop(0, rows, one_row, 0, unroll=4)
    total = None
    for basis in range(basis_count):
        part = lax.dot_general(
            spread[basis].reshape(rows * cols, channels),
            mixing[basis],
            (((1,), (1,)), ((), ())),
            preferred_element_type=F32,
        )
        total = part if total is None else total + part
    out[...] = total.reshape(rows, cols, channels).astype(BF16)


def first_sum_kernel(place, keep, recv, *outs):
    fours = outs[:4]
    eights = outs[4:]
    half = keep.shape[2] // 2
    y, x = place[1], place[2]
    depth = eights[0].shape[1]
    for step in range(4):
        row = 2 * lax.rem(y + step, 4)
        total = keep[pl.ds(row, 2), :, :half] + recv[pl.ds(row, 2), :, :half].astype(F32)
        fours[step][...] = total.astype(fours[step].dtype)
        target = lax.rem(x + step, 4)
        lines = pl.ds(pl.multiple_of(lax.rem(target, 2) * depth, depth), depth)
        for other in range(4):
            pair = 2 * other + target // 2
            total = keep[pair, lines, half:] + recv[pair, lines, half:].astype(F32)
            eights[step][other] = total.astype(eights[step].dtype)


def added(refs):
    total = refs[0][...]
    for ref in refs[1:]:
        total = total + ref[...].astype(F32)
    return total


def second_sum_kernel(place, *refs):
    by_y, by_x = refs[:4], refs[4:8]
    over_x, over_y = refs[8:12], refs[12:16]
    one, two = refs[16:]
    one[...] = added(by_y)
    two[...] = added(by_x)
    y, x = place[1], place[2]
    depth = over_x[0].shape[0]
    for step in range(4):
        target = lax.rem(x + step, 4)
        lines = pl.ds(pl.multiple_of(lax.rem(target, 2) * depth, depth), depth)
        over_x[step][...] = one[target // 2, lines, :].astype(over_x[step].dtype)
        over_y[step][...] = two[lax.rem(y + step, 4)].astype(over_y[step].dtype)


def third_sum_kernel(place, *refs):
    over_x, over_y = refs[:4], refs[4:8]
    keep, send, whole = refs[8:]
    half = over_x[0].shape[1]
    whole[:, :half] = added(over_x)
    whole[:, half:] = added(over_y)
    depth = keep.shape[0]
    odd = lax.rem(place[4], 2)
    keep[...] = whole[pl.ds(pl.multiple_of(odd * depth, depth), depth), :]
    send[...] = whole[pl.ds(pl.multiple_of((1 - odd) * depth, depth), depth), :]


def fourth_sum_kernel(keep, recv, out):
    out[...] = (keep[...] + recv[...]).astype(BF16)


def fifth_sum_kernel(normalizer, one, two, three, four, out):
    near = one[...].astype(F32) + two[...].astype(F32)
    far = three[...].astype(F32) + four[...].astype(F32)
    out[...] = (near + far) * normalizer


def placing_kernel(place, own, by_z, by_x, by_both, out):
    odd = lax.rem(place[4], 2)
    low = lax.rem(place[2], 2)
    out[2 * low + odd] = own[...]
    out[2 * low + 1 - odd] = by_z[...]
    out[2 * (1 - low) + odd] = by_x[...]
    out[2 * (1 - low) + 1 - odd] = by_both[...]


LAT = ("y", "xh", "core")
LON = ("xl", "z")
CROSS = ("xh", "xl")


def shift(cells, axis, count, step):
    return lax.ppermute(cells, axis, [(i, (i + step) % count) for i in range(count)])


def swap(cells, axis, count, mask):
    return lax.ppermute(cells, axis, [(i, i ^ mask) for i in range(count)])


def halo(cells):
    rows, cols, _ = cells.shape
    lons = lax.axis_size(LON)
    lats = lax.axis_size(LAT)
    west = shift(cells[:, cols - WL :], LON, lons, 1)
    east = shift(cells[:, :WL], LON, lons, -1)
    north = lax.ppermute(cells[rows - HL :], LAT, [(i, i + 1) for i in range(lats - 1)])
    south = lax.ppermute(cells[:HL], LAT, [(i + 1, i) for i in range(lats - 1)])
    both = jnp.concatenate([north, south], axis=0)
    rims_w = shift(both[:, cols - WL :], LON, lons, 1)
    rims_e = shift(both[:, :WL], LON, lons, -1)
    return west, east, north, south, rims_w, rims_e


def call(kernel, outs, args, specs, name, scratch=(), flops=0, moved=0):
    return pl.pallas_call(
        kernel,
        out_shape=outs,
        in_specs=specs,
        out_specs=jax.tree.map(lambda _: VMEM, outs),
        scratch_shapes=list(scratch),
        compiler_params=PARAMS,
        cost_estimate=pl.CostEstimate(flops=flops, bytes_accessed=moved, transcendentals=0),
        name=name,
    )(*args)


def shaped(shape, dtype):
    return jax.ShapeDtypeStruct(shape, dtype)


def reduced(place, keep, send, normalizer):
    pairs, lines, channels = keep.shape
    half = channels // 2
    deep = lines // 2
    kinds = [F32, BF16, BF16, BF16]
    recv = swap(send, "core", 2, 1)
    parts = call(
        first_sum_kernel,
        tuple(shaped((2, lines, half), kind) for kind in kinds)
        + tuple(shaped((4, deep, half), kind) for kind in kinds),
        (place, keep, recv),
        [SMEM, VMEM, VMEM],
        "first_sum",
        flops=keep.size * 4,
        moved=keep.size * 8,
    )
    by_y = [parts[0]] + [shift(parts[s], "y", 4, s) for s in (1, 2, 3)]
    by_x = [parts[4]] + [shift(parts[4 + s], CROSS, 4, s) for s in (1, 2, 3)]
    parts = call(
        second_sum_kernel,
        tuple(shaped((deep, half), kind) for kind in kinds + kinds),
        (place, *by_y, *by_x),
        [SMEM] + [VMEM] * 8,
        "second_sum",
        [pltpu.VMEM((2, lines, half), F32), pltpu.VMEM((4, deep, half), F32)],
        flops=keep.size,
        moved=keep.size * 2,
    )
    over_x = [parts[0]] + [shift(parts[s], CROSS, 4, s) for s in (1, 2, 3)]
    over_y = [parts[4]] + [shift(parts[4 + s], "y", 4, s) for s in (1, 2, 3)]
    own, other = call(
        third_sum_kernel,
        (shaped((deep // 2, channels), F32),) * 2,
        (place, *over_x, *over_y),
        [SMEM] + [VMEM] * 8,
        "third_sum",
        [pltpu.VMEM((deep, channels), F32)],
        flops=keep.size // 4,
        moved=keep.size // 2,
    )
    recv = swap(other, "z", 8, 1)
    mine = call(
        fourth_sum_kernel,
        shaped(own.shape, BF16),
        (own, recv),
        [VMEM] * 2,
        "fourth_sum",
        flops=own.size,
        moved=own.size * 8,
    )
    result = call(
        functools.partial(fifth_sum_kernel, normalizer),
        shaped(own.shape, F32),
        (mine, *(swap(mine, "z", 8, mask) for mask in (2, 4, 6))),
        [VMEM] * 4,
        "fifth_sum",
        flops=own.size * 4,
        moved=own.size * 12,
    )
    by_z = swap(result, "z", 8, 1)
    by_x = swap(result, "xl", 2, 1)
    by_both = swap(result, LON, 16, 9)
    return call(
        placing_kernel,
        shaped((4,) + result.shape, F32),
        (place, result, by_z, by_x, by_both),
        [SMEM] + [VMEM] * 4,
        "placing",
        moved=own.size * 32,
    )


def local(field, filter_values, block_lat, block_lon, mixing, cotangent):
    rows, cols, channels = field.shape
    basis_count, _, blocks, taps = filter_values.shape
    field_halo = halo(field)
    cot_halo = halo(cotangent)
    place = jnp.stack(
        [
            lax.axis_index(LAT) * rows,
            lax.axis_index("y"),
            lax.axis_index(CROSS),
            lax.axis_index("core"),
            lax.axis_index("z"),
        ]
    ).astype(jnp.int32)

    psi_lines = filter_values.transpose(2, 0, 3, 1).reshape(blocks, basis_count * taps, -1)
    lat_lines = block_lat.T
    lon_lines = block_lon.T
    bank = jnp.concatenate(
        [psi_lines, lon_lines[:, None].astype(BF16), lat_lines[:, None].astype(BF16)], axis=1
    )
    wide = cols + 2 * WL
    fwd_taps, adj_taps = call(
        taps_kernel,
        (
            shaped((rows, basis_count * cols, blocks * wide), BF16),
            shaped((rows, basis_count * cols, SPAN * wide), BF16),
        ),
        (place, bank),
        [SMEM, VMEM],
        "taps",
        flops=4_000_000_000,
        moved=2_000_000,
    )

    lat_count = lax.axis_size(LAT)
    share = channels // lat_count
    lines = basis_count * share
    keep, send, filtered = call(
        filter_kernel,
        (
            shaped((lat_count // 2, lines, channels), F32),
            shaped((lat_count // 2, lines, channels), BF16),
            shaped((basis_count, rows, cols, channels), BF16),
        ),
        (place, lat_lines, fwd_taps, field, *field_halo, cotangent),
        [SMEM] * 2 + [VMEM] * 9,
        "filtering",
        [pltpu.VMEM((rows + 2 * HL, wide, channels), BF16)],
        flops=2_000_000_000,
        moved=8_000_000,
    )
    output = call(
        output_kernel,
        shaped((rows, cols, channels), BF16),
        (filtered, mixing),
        [VMEM] * 2,
        "mixed",
        flops=1_500_000_000,
        moved=4_500_000,
    )
    field_grad = call(
        adjoint_kernel,
        shaped((rows, cols, channels), BF16),
        (adj_taps, cotangent, *cot_halo, mixing),
        [VMEM] * 9,
        "adjoint",
        [
            pltpu.VMEM((rows + 2 * HL, wide, channels), BF16),
            pltpu.VMEM((basis_count, rows, cols, channels), BF16),
        ],
        flops=3_000_000_000,
        moved=6_000_000,
    )
    normalizer = 1.0 / math.sqrt(rows * lat_count * cols * lax.axis_size(LON))
    return (output, field_grad, reduced(place, keep, send, normalizer))


def solution(mesh):
    grid = Mesh(mesh.devices.reshape(4, 2, 2, 2, 8), ("y", "xh", "core", "xl", "z"))
    return jax.shard_map(
        local,
        mesh=grid,
        in_specs=(P(LAT, LON, None), P(), P(), P(), P(), P(LAT, LON, None)),
        out_specs=(P(LAT, LON, None), P(LAT, LON, None), P(None, LAT, None)),
        check_vma=False,
    )
```

```python
import functools
import math

import jax
import jax.numpy as jnp
from jax import lax
from jax.experimental import pallas as pl
from jax.experimental.pallas import tpu as pltpu
from jax.sharding import Mesh
from jax.sharding import PartitionSpec as P

HL = 2
WL = 16
SPAN = 2 * HL + 1
F32 = jnp.float32
BF16 = jnp.bfloat16
VMEM = pl.BlockSpec(memory_space=pltpu.VMEM)
SMEM = pl.BlockSpec(memory_space=pltpu.SMEM)
PARAMS = pltpu.CompilerParams(vmem_limit_bytes=24 * 1024 * 1024)


def iota(shape, axis):
    return lax.broadcasted_iota(jnp.int32, shape, axis)


def placed_lines(weights, distance, count):
    kinds = iota((weights.shape[0], 1), 0) % count
    return jnp.where(distance == kinds, weights, 0.0)


def store_bands(out, row, lines, basis_count, count, taps):
    cols = out.shape[1] // basis_count
    width = out.shape[2]
    for basis in range(basis_count):
        first = basis * count
        line = lines[first : first + 1]
        for tap in range(1, taps):
            line = line + lines[first + tap : first + tap + 1]
        for lane in range(0, width, 128):
            tile = jnp.broadcast_to(line[:, lane : lane + 128], (cols, 128))
            tile = pltpu.roll(tile, 0, 1, stride=1, stride_axis=0).astype(BF16)
            room = min(128, width - lane)
            out[row, basis * cols : (basis + 1) * cols, lane : lane + room] = tile[:, :room]


def gathered(near_all, place, psi, lat, lon, rows):
    basis_count, blocks, taps, cycles = psi.shape
    lines = basis_count * (taps + 2)
    cycle = iota((cycles, 128), 0) - place[0] + HL
    hot = ((iota((cycles, 128), 1) == cycle) & (cycle < rows + 2 * HL)).astype(BF16)
    for block in range(blocks):
        turns = [lon[block : block + 1].astype(F32), lat[block : block + 1].astype(F32)]
        here = []
        for basis in range(basis_count):
            here += [psi[basis, block].astype(F32)] + turns
        here = jnp.concatenate(here, axis=0).astype(BF16)
        near_all[block * lines : (block + 1) * lines] = jnp.dot(
            here, hot, preferred_element_type=F32
        ).astype(BF16)


def forward_taps_kernel(place, psi, lat, lon, forward, near_all, spread):
    rows = forward.shape[0]
    basis_count, blocks, taps, cycles = psi.shape
    count = taps + 2
    wide = forward.shape[2] // blocks
    lines = basis_count * count
    gathered(near_all, place, psi, lat, lon, rows)
    near = near_all[...]
    slot = iota((128, 128), 0) - HL
    base = iota((1, wide), 1) - WL

    def one_row(row, carry):
        weights_all = jnp.dot(near, (slot == row).astype(BF16), preferred_element_type=F32)
        totals = []
        for block in range(blocks):
            weights = weights_all[block * lines : (block + 1) * lines, :wide]
            distance = base - weights[taps : taps + 1].astype(jnp.int32)
            totals.append(placed_lines(weights, distance, count))
        store_bands(forward, row, jnp.concatenate(totals, axis=1), basis_count, count, taps)
        return carry

    lax.fori_loop(0, rows, one_row, 0, unroll=4)


def adjoint_taps_kernel(place, after, psi, lat, lon, adjoint, near_all, adj_wide):
    rows = adjoint.shape[0]
    basis_count, blocks, taps, cycles = psi.shape
    count = taps + 2
    wide = adjoint.shape[2] // SPAN
    lines = basis_count * count
    gathered(near_all, place, psi, lat, lon, rows)
    near = near_all[...]
    lanes = adj_wide.shape[1]
    slot = iota((128, lanes), 0) - iota((128, lanes), 1) // wide
    inside = iota((128, lanes), 1) // wide < SPAN
    turn = iota((1, lanes), 1)
    wanted = HL - turn // wide
    base = WL - turn % wide

    def one_row(row, carry):
        adj_wide[...] = jnp.dot(
            near, ((slot == row) & inside).astype(BF16), preferred_element_type=F32
        )
        total = None
        for block in range(blocks):
            weights = adj_wide[block * lines : (block + 1) * lines, :]
            shift = weights[taps : taps + 1].astype(jnp.int32)
            match = weights[taps + 1 : taps + 2].astype(jnp.int32) == wanted
            value = placed_lines(weights, base - jnp.where(match, shift, 4 * wide), count)
            total = value if total is None else total + value
        store_bands(adjoint, row, total, basis_count, count, taps)
        return carry

    lax.fori_loop(0, rows, one_row, 0, unroll=2)


def rims_kernel(place, after, inner, outer, to_east, to_west):
    cols = inner.shape[2]
    odd = place[3] == 1
    north = jnp.where(odd, inner[...], outer[...])
    south = jnp.where(odd, outer[...], inner[...])
    to_east[0] = north[:, :, cols - WL :]
    to_east[1] = south[:, :, cols - WL :]
    to_west[0] = north[:, :, :WL]
    to_west[1] = south[:, :, :WL]


def assemble(which, place, extended, center, west, east, inner, outer, rims_w, rims_e):
    rows, cols, _ = center.shape
    extended[HL : HL + rows, 0:WL] = west[...]
    extended[HL : HL + rows, WL : WL + cols] = center[...]
    extended[HL : HL + rows, WL + cols :] = east[...]
    odd = place[3] == 1
    above = place[0] > 0
    below = place[0] + rows < place[5]
    none = jnp.zeros((), BF16)
    north = jnp.where(odd, inner[which], outer[which])
    south = jnp.where(odd, outer[which], inner[which])
    for side, (inside, rim, lines) in enumerate(
        ((above, north, slice(0, HL)), (below, south, slice(HL + rows, None)))
    ):
        extended[lines, 0:WL] = jnp.where(inside, rims_w[side, which], none)
        extended[lines, WL : WL + cols] = jnp.where(inside, rim, none)
        extended[lines, WL + cols :] = jnp.where(inside, rims_e[side, which], none)


def filter_kernel(
    place, lat, taps, center, west, east, inner, outer, rims_w, rims_e, cot, keep, send, filt_out, extended
):
    rows, cols, channels = center.shape
    basis_count = filt_out.shape[0]
    blocks = lat.shape[0]
    assemble(0, place, extended, center, west, east, inner, outer, rims_w, rims_e)

    def one_row(row, carry):
        slabs = [extended[row + HL + lat[block, place[0] + row]] for block in range(blocks)]
        slab = jnp.concatenate(slabs, axis=0)
        filtered = jnp.dot(taps[row], slab, preferred_element_type=F32).astype(BF16)
        filt_out[:, row] = filtered.reshape(basis_count, cols, channels)
        return carry

    lax.fori_loop(0, rows, one_row, 0, unroll=4)
    cot_flat = cot[...].reshape(rows * cols, channels)
    pairs = keep.shape[0] // 2
    share = channels // (2 * pairs)
    per = keep.shape[1] // share
    core = place[3]
    for basis in range(basis_count):
        filtered = filt_out[basis].reshape(rows * cols, channels)
        terms = lax.dot_general(
            filtered, cot_flat, (((0,), (0,)), ((), ())), preferred_element_type=F32
        ).reshape(pairs, 2, share, channels)
        lines = slice(basis % per * share, (basis % per + 1) * share)
        mine = jnp.where(core == 0, terms[:, 0], terms[:, 1])
        other = jnp.where(core == 0, terms[:, 1], terms[:, 0]).astype(BF16)
        for pair in range(pairs):
            keep[2 * pair + basis // per, lines] = mine[pair]
            send[2 * pair + basis // per, lines] = other[pair]


def output_kernel(filt, mixing, out, token):
    token[...] = jnp.zeros_like(token)
    basis_count, rows, cols, channels = filt.shape
    total = None
    for basis in range(basis_count):
        part = jnp.dot(
            filt[basis].reshape(rows * cols, channels), mixing[basis], preferred_element_type=F32
        )
        total = part if total is None else total + part
    out[...] = total.reshape(rows, cols, channels).astype(BF16)


def adjoint_kernel(
    place, after, taps, center, west, east, inner, outer, rims_w, rims_e, mixing, out, token, extended, spread
):
    token[...] = jnp.zeros_like(token)
    rows, cols, channels = center.shape
    basis_count = mixing.shape[0]
    assemble(1, place, extended, center, west, east, inner, outer, rims_w, rims_e)

    def one_row(row, carry):
        slab = extended[pl.ds(row, SPAN)].reshape(SPAN * (cols + 2 * WL), channels)
        pulled = jnp.dot(taps[row], slab, preferred_element_type=F32).astype(BF16)
        spread[:, row] = pulled.reshape(basis_count, cols, channels)
        return carry

    lax.fori_loop(0, rows, one_row, 0, unroll=4)
    total = None
    for basis in range(basis_count):
        part = lax.dot_general(
            spread[basis].reshape(rows * cols, channels),
            mixing[basis],
            (((1,), (1,)), ((), ())),
            preferred_element_type=F32,
        )
        total = part if total is None else total + part
    out[...] = total.reshape(rows, cols, channels).astype(BF16)


def pair_sum_kernel(after, keep, recv, out):
    out[...] = (keep[...] + recv[...].astype(F32)).astype(BF16)


def chip_sum_kernel(after, parts, out):
    total = parts[0].astype(F32)
    for chip in range(1, parts.shape[0]):
        total = total + parts[chip].astype(F32)
    out[...] = total.astype(BF16)


def four_sum_kernel(one, two, three, four, out):
    near = one[...].astype(F32) + two[...].astype(F32)
    far = three[...].astype(F32) + four[...].astype(F32)
    out[...] = (near + far).astype(BF16)


def last_sum_kernel(normalizer, place, own, by_z, by_x, by_both, out):
    low = lax.rem(place[2], 2)
    shape = (2,) + out.shape[1:]
    mine = own[...].astype(F32) + by_z[...].astype(F32)
    other = by_x[...].astype(F32) + by_both[...].astype(F32)
    out[pl.ds(2 * low, 2)] = (mine * normalizer).reshape(shape)
    out[pl.ds(2 * (1 - low), 2)] = (other * normalizer).reshape(shape)


LAT = ("y", "xh", "core")
LON = ("xl", "z")
CROSS = ("xh", "xl")


def shift(cells, axis, count, step):
    return lax.ppermute(cells, axis, [(i, (i + step) % count) for i in range(count)])


def swap(cells, axis, count, mask):
    return lax.ppermute(cells, axis, [(i, i ^ mask) for i in range(count)])


def call(kernel, outs, args, specs, name, scratch=(), flops=0, moved=0):
    return pl.pallas_call(
        kernel,
        out_shape=outs,
        in_specs=specs,
        out_specs=jax.tree.map(lambda _: VMEM, outs),
        scratch_shapes=list(scratch),
        compiler_params=PARAMS,
        cost_estimate=pl.CostEstimate(flops=flops, bytes_accessed=moved, transcendentals=0),
        name=name,
    )(*args)


def shaped(shape, dtype):
    return jax.ShapeDtypeStruct(shape, dtype)


def local(field, filter_values, block_lat, block_lon, mixing, cotangent):
    rows, cols, channels = field.shape
    basis_count, _, blocks, taps = filter_values.shape
    lats = lax.axis_size(LAT)
    lons = lax.axis_size(LON)
    place = jnp.stack(
        [
            lax.axis_index(LAT) * rows,
            lax.axis_index("y"),
            lax.axis_index(CROSS),
            lax.axis_index("core"),
            lax.axis_index("z"),
            jnp.int32(rows * lats),
        ]
    ).astype(jnp.int32)
    both = (field, cotangent)
    odd = lax.axis_index("core") == 1
    top = jnp.stack([cells[:HL] for cells in both])
    bottom = jnp.stack([cells[rows - HL :] for cells in both])
    inner = jnp.where(odd, top, bottom)
    outer = jnp.where(odd, bottom, top)
    west = shift(field[:, cols - WL :], LON, lons, 1)
    east = shift(field[:, :WL], LON, lons, -1)
    psi = filter_values.transpose(0, 2, 3, 1)
    lat = block_lat.T
    lon = block_lon.T
    wide = cols + 2 * WL
    lines = basis_count * blocks * (taps + 2)
    fwd_taps = call(
        forward_taps_kernel,
        shaped((rows, basis_count * cols, blocks * wide), BF16),
        (place, psi, lat, lon),
        [SMEM] + [VMEM] * 3,
        "forward_taps",
        [pltpu.VMEM((lines, 128), BF16), pltpu.VMEM((lines, 128), F32)],
        flops=1_000_000_000,
        moved=1_000_000,
    )
    inner = swap(inner, LAT, lats, 1)
    pairs = [(0, 0), (lats - 1, lats - 1)]
    for low in range(1, lats - 1, 2):
        pairs += [(low, low + 1), (low + 1, low)]
    outer = lax.ppermute(outer, LAT, pairs)
    rim = shaped((2, 2, HL, WL, channels), BF16)
    rim_to_east, rim_to_west = call(
        rims_kernel,
        (rim, rim),
        (place, fwd_taps, inner, outer),
        [SMEM] + [VMEM] * 3,
        "rims",
        moved=1_000_000,
    )
    rims_w = shift(rim_to_east, LON, lons, 1)
    rims_e = shift(rim_to_west, LON, lons, -1)
    share = basis_count * channels // lats
    keep, send, filtered = call(
        filter_kernel,
        (
            shaped((lats, share // 2, channels), F32),
            shaped((lats, share // 2, channels), BF16),
            shaped((basis_count, rows, cols, channels), BF16),
        ),
        (place, lat, fwd_taps, field, west, east, inner, outer, rims_w, rims_e, cotangent),
        [SMEM] * 2 + [VMEM] * 9,
        "filtering",
        [pltpu.VMEM((rows + 2 * HL, wide, channels), BF16)],
        flops=2_000_000_000,
        moved=8_000_000,
    )
    recv = swap(send, "core", 2, 1)
    cot_west = shift(cotangent[:, cols - WL :], LON, lons, 1)
    cot_east = shift(cotangent[:, :WL], LON, lons, -1)
    token = shaped((8, 128), F32)
    output, token_one = call(
        output_kernel,
        (shaped((rows, cols, channels), BF16), token),
        (filtered, mixing),
        [VMEM] * 2,
        "mixed",
        flops=1_500_000_000,
        moved=4_500_000,
    )
    summed = call(
        pair_sum_kernel,
        shaped(keep.shape, BF16),
        (token_one, keep, recv),
        [VMEM] * 3,
        "pair_sum",
        flops=keep.size,
        moved=keep.size * 8,
    )
    parts = lax.all_to_all(summed, ("y", "xh", "xl"), 0, 0)

    adj_taps = call(
        adjoint_taps_kernel,
        shaped((rows, basis_count * cols, SPAN * wide), BF16),
        (place, summed, psi, lat, lon),
        [SMEM] + [VMEM] * 4,
        "adjoint_taps",
        [
            pltpu.VMEM((lines, 128), BF16),
            pltpu.VMEM((lines, -(-SPAN * wide // 128) * 128), F32),
        ],
        flops=2_000_000_000,
        moved=2_000_000,
    )
    field_grad, token_two = call(
        adjoint_kernel,
        (shaped((rows, cols, channels), BF16), token),
        (
            place,
            summed,
            adj_taps,
            cotangent,
            cot_west,
            cot_east,
            inner,
            outer,
            rims_w,
            rims_e,
            mixing,
        ),
        [SMEM, VMEM] + [VMEM] * 9,
        "adjoint",
        [
            pltpu.VMEM((rows + 2 * HL, wide, channels), BF16),
            pltpu.VMEM((basis_count, rows, cols, channels), BF16),
        ],
        flops=3_000_000_000,
        moved=6_000_000,
    )

    _, deep, _ = parts.shape
    part = call(
        chip_sum_kernel,
        shaped((deep, channels), BF16),
        (token_two, parts),
        [VMEM] * 2,
        "chip_sum",
        flops=parts.size,
        moved=parts.size * 2,
    )
    part = call(
        four_sum_kernel,
        shaped((deep, channels), BF16),
        (part, *(swap(part, "z", 8, mask) for mask in (2, 4, 6))),
        [VMEM] * 4,
        "four_sum",
        flops=part.size * 4,
        moved=part.size * 10,
    )
    normalizer = 1.0 / math.sqrt(rows * lats * cols * lons)
    mixing_grad = call(
        functools.partial(last_sum_kernel, normalizer),
        shaped((basis_count, channels // lats, channels), F32),
        (place, part, swap(part, "z", 8, 1), swap(part, "xl", 2, 1), swap(part, LON, 16, 9)),
        [SMEM] + [VMEM] * 4,
        "last_sum",
        flops=part.size * 4,
        moved=part.size * 16,
    )
    return (output, field_grad, mixing_grad)


def solution(mesh):
    grid = Mesh(mesh.devices.reshape(4, 2, 2, 2, 8), ("y", "xh", "core", "xl", "z"))
    return jax.shard_map(
        local,
        mesh=grid,
        in_specs=(P(LAT, LON, None), P(), P(), P(), P(), P(LAT, LON, None)),
        out_specs=(P(LAT, LON, None), P(LAT, LON, None), P(None, LAT, None)),
        check_vma=False,
    )
```

```python
import functools
import math

import jax
import jax.numpy as jnp
from jax import lax
from jax.experimental import pallas as pl
from jax.experimental.pallas import tpu as pltpu
from jax.sharding import Mesh
from jax.sharding import PartitionSpec as P

HL = 2
MIXED_COST = 60_000_000_000
FILTER_COST = 20_000_000_000
WL = 16
SPAN = 2 * HL + 1
F32 = jnp.float32
BF16 = jnp.bfloat16
VMEM = pl.BlockSpec(memory_space=pltpu.VMEM)
SMEM = pl.BlockSpec(memory_space=pltpu.SMEM)
PARAMS = pltpu.CompilerParams(vmem_limit_bytes=24 * 1024 * 1024)


def iota(shape, axis):
    return lax.broadcasted_iota(jnp.int32, shape, axis)


def placed_lines(weights, distance, count):
    kinds = iota((weights.shape[0], 1), 0) % count
    return jnp.where(distance == kinds, weights, 0.0)


def store_bands(out, row, lines, basis_count, count, taps):
    cols = out.shape[1] // basis_count
    width = out.shape[2]
    for basis in range(basis_count):
        first = basis * count
        line = lines[first : first + 1]
        for tap in range(1, taps):
            line = line + lines[first + tap : first + tap + 1]
        for lane in range(0, width, 128):
            tile = jnp.broadcast_to(line[:, lane : lane + 128], (cols, 128))
            tile = pltpu.roll(tile, 0, 1, stride=1, stride_axis=0).astype(BF16)
            room = min(128, width - lane)
            out[row, basis * cols : (basis + 1) * cols, lane : lane + room] = tile[:, :room]


def gathered(near_all, place, psi, lat, lon, rows):
    basis_count, blocks, taps, cycles = psi.shape
    lines = basis_count * (taps + 2)
    cycle = iota((cycles, 128), 0) - place[0] + HL
    hot = ((iota((cycles, 128), 1) == cycle) & (cycle < rows + 2 * HL)).astype(BF16)
    for block in range(blocks):
        turns = [lon[block : block + 1].astype(F32), lat[block : block + 1].astype(F32)]
        here = []
        for basis in range(basis_count):
            here += [psi[basis, block].astype(F32)] + turns
        here = jnp.concatenate(here, axis=0).astype(BF16)
        near_all[block * lines : (block + 1) * lines] = jnp.dot(
            here, hot, preferred_element_type=F32
        ).astype(BF16)


def forward_taps_kernel(place, psi, lat, lon, forward, near_all, spread):
    rows = forward.shape[0]
    basis_count, blocks, taps, cycles = psi.shape
    count = taps + 2
    wide = forward.shape[2] // blocks
    lines = basis_count * count
    gathered(near_all, place, psi, lat, lon, rows)
    near = near_all[...]
    slot = iota((128, 128), 0) - HL
    base = iota((1, wide), 1) - WL

    def one_row(row, carry):
        weights_all = jnp.dot(near, (slot == row).astype(BF16), preferred_element_type=F32)
        totals = []
        for block in range(blocks):
            weights = weights_all[block * lines : (block + 1) * lines, :wide]
            distance = base - weights[taps : taps + 1].astype(jnp.int32)
            totals.append(placed_lines(weights, distance, count))
        store_bands(forward, row, jnp.concatenate(totals, axis=1), basis_count, count, taps)
        return carry

    lax.fori_loop(0, rows, one_row, 0, unroll=4)


def adjoint_taps_kernel(place, after, psi, lat, lon, adjoint, near_all, adj_wide):
    rows = adjoint.shape[0]
    basis_count, blocks, taps, cycles = psi.shape
    count = taps + 2
    wide = adjoint.shape[2] // SPAN
    lines = basis_count * count
    gathered(near_all, place, psi, lat, lon, rows)
    near = near_all[...]
    lanes = adj_wide.shape[1]
    slot = iota((128, lanes), 0) - iota((128, lanes), 1) // wide
    inside = iota((128, lanes), 1) // wide < SPAN
    turn = iota((1, lanes), 1)
    wanted = HL - turn // wide
    base = WL - turn % wide

    def one_row(row, carry):
        adj_wide[...] = jnp.dot(
            near, ((slot == row) & inside).astype(BF16), preferred_element_type=F32
        )
        total = None
        for block in range(blocks):
            weights = adj_wide[block * lines : (block + 1) * lines, :]
            shift = weights[taps : taps + 1].astype(jnp.int32)
            match = weights[taps + 1 : taps + 2].astype(jnp.int32) == wanted
            value = placed_lines(weights, base - jnp.where(match, shift, 4 * wide), count)
            total = value if total is None else total + value
        store_bands(adjoint, row, total, basis_count, count, taps)
        return carry

    lax.fori_loop(0, rows, one_row, 0, unroll=2)


def rims_kernel(place, after, inner, outer, cot, to_east, to_west, cot_to_east, cot_to_west):
    cot_to_east[...] = cot[:, cot.shape[1] - WL :]
    cot_to_west[...] = cot[:, :WL]
    cols = inner.shape[2]
    odd = place[3] == 1
    north = jnp.where(odd, inner[...], outer[...])
    south = jnp.where(odd, outer[...], inner[...])
    to_east[0] = north[:, :, cols - WL :]
    to_east[1] = south[:, :, cols - WL :]
    to_west[0] = north[:, :, :WL]
    to_west[1] = south[:, :, :WL]


def assemble(which, place, extended, center, west, east, inner, outer, rims_w, rims_e):
    rows, cols, _ = center.shape
    extended[HL : HL + rows, 0:WL] = west[...]
    extended[HL : HL + rows, WL : WL + cols] = center[...]
    extended[HL : HL + rows, WL + cols :] = east[...]
    odd = place[3] == 1
    above = place[0] > 0
    below = place[0] + rows < place[5]
    none = jnp.zeros((), BF16)
    north = jnp.where(odd, inner[which], outer[which])
    south = jnp.where(odd, outer[which], inner[which])
    for side, (inside, rim, lines) in enumerate(
        ((above, north, slice(0, HL)), (below, south, slice(HL + rows, None)))
    ):
        extended[lines, 0:WL] = jnp.where(inside, rims_w[side, which], none)
        extended[lines, WL : WL + cols] = jnp.where(inside, rim, none)
        extended[lines, WL + cols :] = jnp.where(inside, rims_e[side, which], none)


def filter_kernel(
    place, lat, taps, center, west, east, inner, outer, rims_w, rims_e, cot, keep, send, filt_out, extended
):
    rows, cols, channels = center.shape
    basis_count = filt_out.shape[0]
    blocks = lat.shape[0]
    assemble(0, place, extended, center, west, east, inner, outer, rims_w, rims_e)

    def one_row(row, carry):
        slabs = [extended[row + HL + lat[block, place[0] + row]] for block in range(blocks)]
        slab = jnp.concatenate(slabs, axis=0)
        filtered = jnp.dot(taps[row], slab, preferred_element_type=F32).astype(BF16)
        filt_out[:, row] = filtered.reshape(basis_count, cols, channels)
        return carry

    lax.fori_loop(0, rows, one_row, 0, unroll=4)
    cot_flat = cot[...].reshape(rows * cols, channels)
    pairs = keep.shape[0] // 2
    share = channels // (2 * pairs)
    per = keep.shape[1] // share
    core = place[3]
    for basis in range(basis_count):
        filtered = filt_out[basis].reshape(rows * cols, channels)
        terms = lax.dot_general(
            filtered, cot_flat, (((0,), (0,)), ((), ())), preferred_element_type=F32
        ).reshape(pairs, 2, share, channels)
        lines = slice(basis % per * share, (basis % per + 1) * share)
        mine = jnp.where(core == 0, terms[:, 0], terms[:, 1])
        other = jnp.where(core == 0, terms[:, 1], terms[:, 0]).astype(BF16)
        for pair in range(pairs):
            keep[2 * pair + basis // per, lines] = mine[pair]
            send[2 * pair + basis // per, lines] = other[pair]


def output_kernel(ready_w, ready_e, filt, mixing, out, token):
    token[...] = jnp.zeros_like(token)
    basis_count, rows, cols, channels = filt.shape
    total = None
    for basis in range(basis_count):
        part = jnp.dot(
            filt[basis].reshape(rows * cols, channels), mixing[basis], preferred_element_type=F32
        )
        total = part if total is None else total + part
    out[...] = total.reshape(rows, cols, channels).astype(BF16)


def adjoint_kernel(
    place, after, taps, center, west, east, inner, outer, rims_w, rims_e, mixing, out, token, extended, spread
):
    token[...] = jnp.zeros_like(token)
    rows, cols, channels = center.shape
    basis_count = mixing.shape[0]
    assemble(1, place, extended, center, west, east, inner, outer, rims_w, rims_e)

    def one_row(row, carry):
        slab = extended[pl.ds(row, SPAN)].reshape(SPAN * (cols + 2 * WL), channels)
        pulled = jnp.dot(taps[row], slab, preferred_element_type=F32).astype(BF16)
        spread[:, row] = pulled.reshape(basis_count, cols, channels)
        return carry

    lax.fori_loop(0, rows, one_row, 0, unroll=4)
    total = None
    for basis in range(basis_count):
        part = lax.dot_general(
            spread[basis].reshape(rows * cols, channels),
            mixing[basis],
            (((1,), (1,)), ((), ())),
            preferred_element_type=F32,
        )
        total = part if total is None else total + part
    out[...] = total.reshape(rows, cols, channels).astype(BF16)


def pair_sum_kernel(after, keep, recv, out):
    out[...] = (keep[...] + recv[...].astype(F32)).astype(BF16)


def chip_sum_kernel(after, parts, out):
    total = parts[0].astype(F32)
    for chip in range(1, parts.shape[0]):
        total = total + parts[chip].astype(F32)
    out[...] = total.astype(BF16)


def four_sum_kernel(one, two, three, four, out):
    near = one[...].astype(F32) + two[...].astype(F32)
    far = three[...].astype(F32) + four[...].astype(F32)
    out[...] = (near + far).astype(BF16)


def last_sum_kernel(normalizer, place, own, by_z, by_x, by_both, out):
    low = lax.rem(place[2], 2)
    shape = (2,) + out.shape[1:]
    mine = own[...].astype(F32) + by_z[...].astype(F32)
    other = by_x[...].astype(F32) + by_both[...].astype(F32)
    out[pl.ds(2 * low, 2)] = (mine * normalizer).reshape(shape)
    out[pl.ds(2 * (1 - low), 2)] = (other * normalizer).reshape(shape)


LAT = ("y", "xh", "core")
LON = ("xl", "z")
CROSS = ("xh", "xl")


def shift(cells, axis, count, step):
    return lax.ppermute(cells, axis, [(i, (i + step) % count) for i in range(count)])


def swap(cells, axis, count, mask):
    return lax.ppermute(cells, axis, [(i, i ^ mask) for i in range(count)])


def call(kernel, outs, args, specs, name, scratch=(), flops=0, moved=0):
    return pl.pallas_call(
        kernel,
        out_shape=outs,
        in_specs=specs,
        out_specs=jax.tree.map(lambda _: VMEM, outs),
        scratch_shapes=list(scratch),
        compiler_params=PARAMS,
        cost_estimate=pl.CostEstimate(flops=flops, bytes_accessed=moved, transcendentals=0),
        name=name,
    )(*args)


def shaped(shape, dtype):
    return jax.ShapeDtypeStruct(shape, dtype)


def local(field, filter_values, block_lat, block_lon, mixing, cotangent):
    rows, cols, channels = field.shape
    basis_count, _, blocks, taps = filter_values.shape
    lats = lax.axis_size(LAT)
    lons = lax.axis_size(LON)
    place = jnp.stack(
        [
            lax.axis_index(LAT) * rows,
            lax.axis_index("y"),
            lax.axis_index(CROSS),
            lax.axis_index("core"),
            lax.axis_index("z"),
            jnp.int32(rows * lats),
        ]
    ).astype(jnp.int32)
    both = (field, cotangent)
    odd = lax.axis_index("core") == 1
    top = jnp.stack([cells[:HL] for cells in both])
    bottom = jnp.stack([cells[rows - HL :] for cells in both])
    inner = jnp.where(odd, top, bottom)
    outer = jnp.where(odd, bottom, top)
    west = shift(field[:, cols - WL :], LON, lons, 1)
    east = shift(field[:, :WL], LON, lons, -1)
    psi = filter_values.transpose(0, 2, 3, 1)
    lat = block_lat.T
    lon = block_lon.T
    wide = cols + 2 * WL
    lines = basis_count * blocks * (taps + 2)
    fwd_taps = call(
        forward_taps_kernel,
        shaped((rows, basis_count * cols, blocks * wide), BF16),
        (place, psi, lat, lon),
        [SMEM] + [VMEM] * 3,
        "forward_taps",
        [pltpu.VMEM((lines, 128), BF16), pltpu.VMEM((lines, 128), F32)],
        flops=1_000_000_000,
        moved=1_000_000,
    )
    inner = swap(inner, LAT, lats, 1)
    pairs = [(0, 0), (lats - 1, lats - 1)]
    for low in range(1, lats - 1, 2):
        pairs += [(low, low + 1), (low + 1, low)]
    outer = lax.ppermute(outer, LAT, pairs)
    rim = shaped((2, 2, HL, WL, channels), BF16)
    side = shaped((rows, WL, channels), BF16)
    rim_to_east, rim_to_west, cot_to_east, cot_to_west = call(
        rims_kernel,
        (rim, rim, side, side),
        (place, fwd_taps, inner, outer, cotangent),
        [SMEM] + [VMEM] * 4,
        "rims",
        moved=1_000_000,
    )
    rims_w = shift(rim_to_east, LON, lons, 1)
    rims_e = shift(rim_to_west, LON, lons, -1)
    share = basis_count * channels // lats
    keep, send, filtered = call(
        filter_kernel,
        (
            shaped((lats, share // 2, channels), F32),
            shaped((lats, share // 2, channels), BF16),
            shaped((basis_count, rows, cols, channels), BF16),
        ),
        (place, lat, fwd_taps, field, west, east, inner, outer, rims_w, rims_e, cotangent),
        [SMEM] * 2 + [VMEM] * 9,
        "filtering",
        [pltpu.VMEM((rows + 2 * HL, wide, channels), BF16)],
        flops=FILTER_COST,
        moved=8_000_000,
    )
    recv = swap(send, "core", 2, 1)
    cot_west = shift(cot_to_east, LON, lons, 1)
    cot_east = shift(cot_to_west, LON, lons, -1)
    token = shaped((8, 128), F32)
    output, token_one = call(
        output_kernel,
        (shaped((rows, cols, channels), BF16), token),
        (cot_west, cot_east, filtered, mixing),
        [VMEM] * 4,
        "mixed",
        flops=MIXED_COST,
        moved=4_500_000,
    )
    summed = call(
        pair_sum_kernel,
        shaped(keep.shape, BF16),
        (token_one, keep, recv),
        [VMEM] * 3,
        "pair_sum",
        flops=keep.size,
        moved=keep.size * 8,
    )
    parts = lax.all_to_all(summed, ("y", "xh", "xl"), 0, 0)

    adj_taps = call(
        adjoint_taps_kernel,
        shaped((rows, basis_count * cols, SPAN * wide), BF16),
        (place, summed, psi, lat, lon),
        [SMEM] + [VMEM] * 4,
        "adjoint_taps",
        [
            pltpu.VMEM((lines, 128), BF16),
            pltpu.VMEM((lines, -(-SPAN * wide // 128) * 128), F32),
        ],
        flops=2_000_000_000,
        moved=2_000_000,
    )
    field_grad, token_two = call(
        adjoint_kernel,
        (shaped((rows, cols, channels), BF16), token),
        (
            place,
            summed,
            adj_taps,
            cotangent,
            cot_west,
            cot_east,
            inner,
            outer,
            rims_w,
            rims_e,
            mixing,
        ),
        [SMEM, VMEM] + [VMEM] * 9,
        "adjoint",
        [
            pltpu.VMEM((rows + 2 * HL, wide, channels), BF16),
            pltpu.VMEM((basis_count, rows, cols, channels), BF16),
        ],
        flops=3_000_000_000,
        moved=6_000_000,
    )

    _, deep, _ = parts.shape
    part = call(
        chip_sum_kernel,
        shaped((deep, channels), BF16),
        (token_two, parts),
        [VMEM] * 2,
        "chip_sum",
        flops=parts.size,
        moved=parts.size * 2,
    )
    part = call(
        four_sum_kernel,
        shaped((deep, channels), BF16),
        (part, *(swap(part, "z", 8, mask) for mask in (2, 4, 6))),
        [VMEM] * 4,
        "four_sum",
        flops=part.size * 4,
        moved=part.size * 10,
    )
    normalizer = 1.0 / math.sqrt(rows * lats * cols * lons)
    mixing_grad = call(
        functools.partial(last_sum_kernel, normalizer),
        shaped((basis_count, channels // lats, channels), F32),
        (place, part, swap(part, "z", 8, 1), swap(part, "xl", 2, 1), swap(part, LON, 16, 9)),
        [SMEM] + [VMEM] * 4,
        "last_sum",
        flops=part.size * 4,
        moved=part.size * 16,
    )
    return (output, field_grad, mixing_grad)


def solution(mesh):
    grid = Mesh(mesh.devices.reshape(4, 2, 2, 2, 8), ("y", "xh", "core", "xl", "z"))
    return jax.shard_map(
        local,
        mesh=grid,
        in_specs=(P(LAT, LON, None), P(), P(), P(), P(), P(LAT, LON, None)),
        out_specs=(P(LAT, LON, None), P(LAT, LON, None), P(None, LAT, None)),
        check_vma=False,
    )
```

```python
import functools
import math

import jax
import jax.numpy as jnp
from jax import lax
from jax.experimental import pallas as pl
from jax.experimental.pallas import tpu as pltpu
from jax.sharding import Mesh
from jax.sharding import PartitionSpec as P

HL = 2
MIXED_COST = 60_000_000_000
FILTER_COST = 20_000_000_000
WL = 16
SPAN = 2 * HL + 1
F32 = jnp.float32
BF16 = jnp.bfloat16
VMEM = pl.BlockSpec(memory_space=pltpu.VMEM)
SMEM = pl.BlockSpec(memory_space=pltpu.SMEM)
PARAMS = pltpu.CompilerParams(vmem_limit_bytes=24 * 1024 * 1024)


def iota(shape, axis):
    return lax.broadcasted_iota(jnp.int32, shape, axis)


def placed_lines(weights, distance, count):
    kinds = iota((weights.shape[0], 1), 0) % count
    return jnp.where(distance == kinds, weights, 0.0)


def store_bands(out, row, lines, basis_count, count, taps):
    cols = out.shape[1] // basis_count
    width = out.shape[2]
    for basis in range(basis_count):
        first = basis * count
        line = lines[first : first + 1]
        for tap in range(1, taps):
            line = line + lines[first + tap : first + tap + 1]
        for lane in range(0, width, 128):
            tile = jnp.broadcast_to(line[:, lane : lane + 128], (cols, 128))
            tile = pltpu.roll(tile, 0, 1, stride=1, stride_axis=0).astype(BF16)
            room = min(128, width - lane)
            out[row, basis * cols : (basis + 1) * cols, lane : lane + room] = tile[:, :room]


def gathered(near_all, place, psi, lat, lon, rows):
    basis_count, blocks, taps, cycles = psi.shape
    lines = basis_count * (taps + 2)
    cycle = iota((cycles, 128), 0) - place[0] + HL
    hot = ((iota((cycles, 128), 1) == cycle) & (cycle < rows + 2 * HL)).astype(BF16)
    for block in range(blocks):
        turns = [lon[block : block + 1].astype(F32), lat[block : block + 1].astype(F32)]
        here = []
        for basis in range(basis_count):
            here += [psi[basis, block].astype(F32)] + turns
        here = jnp.concatenate(here, axis=0).astype(BF16)
        near_all[block * lines : (block + 1) * lines] = jnp.dot(
            here, hot, preferred_element_type=F32
        ).astype(BF16)


def forward_taps_kernel(place, psi, lat, lon, forward, near_all, spread):
    rows = forward.shape[0]
    basis_count, blocks, taps, cycles = psi.shape
    count = taps + 2
    wide = forward.shape[2] // blocks
    lines = basis_count * count
    gathered(near_all, place, psi, lat, lon, rows)
    near = near_all[...]
    slot = iota((128, 128), 0) - HL
    base = iota((1, wide), 1) - WL

    def one_row(row, carry):
        weights_all = jnp.dot(near, (slot == row).astype(BF16), preferred_element_type=F32)
        totals = []
        for block in range(blocks):
            weights = weights_all[block * lines : (block + 1) * lines, :wide]
            distance = base - weights[taps : taps + 1].astype(jnp.int32)
            totals.append(placed_lines(weights, distance, count))
        store_bands(forward, row, jnp.concatenate(totals, axis=1), basis_count, count, taps)
        return carry

    lax.fori_loop(0, rows, one_row, 0, unroll=16)


def adjoint_taps_kernel(place, after, psi, lat, lon, adjoint, near_all, adj_wide):
    rows = adjoint.shape[0]
    basis_count, blocks, taps, cycles = psi.shape
    count = taps + 2
    wide = adjoint.shape[2] // SPAN
    lines = basis_count * count
    gathered(near_all, place, psi, lat, lon, rows)
    near = near_all[...]
    lanes = adj_wide.shape[1]
    slot = iota((128, lanes), 0) - iota((128, lanes), 1) // wide
    inside = iota((128, lanes), 1) // wide < SPAN
    turn = iota((1, lanes), 1)
    wanted = HL - turn // wide
    base = WL - turn % wide

    def one_row(row, carry):
        adj_wide[...] = jnp.dot(
            near, ((slot == row) & inside).astype(BF16), preferred_element_type=F32
        )
        total = None
        for block in range(blocks):
            weights = adj_wide[block * lines : (block + 1) * lines, :]
            shift = weights[taps : taps + 1].astype(jnp.int32)
            match = weights[taps + 1 : taps + 2].astype(jnp.int32) == wanted
            value = placed_lines(weights, base - jnp.where(match, shift, 4 * wide), count)
            total = value if total is None else total + value
        store_bands(adjoint, row, total, basis_count, count, taps)
        return carry

    lax.fori_loop(0, rows, one_row, 0, unroll=4)


def rims_kernel(place, after, inner, outer, cot, to_east, to_west, cot_to_east, cot_to_west):
    cot_to_east[...] = cot[:, cot.shape[1] - WL :]
    cot_to_west[...] = cot[:, :WL]
    cols = inner.shape[2]
    odd = place[3] == 1
    north = jnp.where(odd, inner[...], outer[...])
    south = jnp.where(odd, outer[...], inner[...])
    to_east[0] = north[:, :, cols - WL :]
    to_east[1] = south[:, :, cols - WL :]
    to_west[0] = north[:, :, :WL]
    to_west[1] = south[:, :, :WL]


def assemble(which, place, extended, center, west, east, inner, outer, rims_w, rims_e):
    rows, cols, _ = center.shape
    extended[HL : HL + rows, 0:WL] = west[...]
    extended[HL : HL + rows, WL : WL + cols] = center[...]
    extended[HL : HL + rows, WL + cols :] = east[...]
    odd = place[3] == 1
    above = place[0] > 0
    below = place[0] + rows < place[5]
    none = jnp.zeros((), BF16)
    north = jnp.where(odd, inner[which], outer[which])
    south = jnp.where(odd, outer[which], inner[which])
    for side, (inside, rim, lines) in enumerate(
        ((above, north, slice(0, HL)), (below, south, slice(HL + rows, None)))
    ):
        extended[lines, 0:WL] = jnp.where(inside, rims_w[side, which], none)
        extended[lines, WL : WL + cols] = jnp.where(inside, rim, none)
        extended[lines, WL + cols :] = jnp.where(inside, rims_e[side, which], none)


def filter_kernel(
    place, lat, taps, center, west, east, inner, outer, rims_w, rims_e, cot, keep, send, filt_out, extended
):
    rows, cols, channels = center.shape
    basis_count = filt_out.shape[0]
    blocks = lat.shape[0]
    assemble(0, place, extended, center, west, east, inner, outer, rims_w, rims_e)

    def one_row(row, carry):
        slabs = [extended[row + HL + lat[block, place[0] + row]] for block in range(blocks)]
        slab = jnp.concatenate(slabs, axis=0)
        filtered = jnp.dot(taps[row], slab, preferred_element_type=F32).astype(BF16)
        filt_out[:, row] = filtered.reshape(basis_count, cols, channels)
        return carry

    lax.fori_loop(0, rows, one_row, 0, unroll=16)
    cot_flat = cot[...].reshape(rows * cols, channels)
    pairs = keep.shape[0] // 2
    share = channels // (2 * pairs)
    per = keep.shape[1] // share
    core = place[3]
    for basis in range(basis_count):
        filtered = filt_out[basis].reshape(rows * cols, channels)
        terms = lax.dot_general(
            filtered, cot_flat, (((0,), (0,)), ((), ())), preferred_element_type=F32
        ).reshape(pairs, 2, share, channels)
        lines = slice(basis % per * share, (basis % per + 1) * share)
        mine = jnp.where(core == 0, terms[:, 0], terms[:, 1])
        other = jnp.where(core == 0, terms[:, 1], terms[:, 0]).astype(BF16)
        for pair in range(pairs):
            keep[2 * pair + basis // per, lines] = mine[pair]
            send[2 * pair + basis // per, lines] = other[pair]


def output_kernel(filt, mixing, out, token):
    token[...] = jnp.zeros_like(token)
    basis_count, rows, cols, channels = filt.shape
    total = None
    for basis in range(basis_count):
        part = jnp.dot(
            filt[basis].reshape(rows * cols, channels), mixing[basis], preferred_element_type=F32
        )
        total = part if total is None else total + part
    out[...] = total.reshape(rows, cols, channels).astype(BF16)


def adjoint_kernel(
    place, after, taps, center, west, east, inner, outer, rims_w, rims_e, mixing, out, token, extended, spread
):
    token[...] = jnp.zeros_like(token)
    rows, cols, channels = center.shape
    basis_count = mixing.shape[0]
    assemble(1, place, extended, center, west, east, inner, outer, rims_w, rims_e)

    def one_row(row, carry):
        slab = extended[pl.ds(row, SPAN)].reshape(SPAN * (cols + 2 * WL), channels)
        pulled = jnp.dot(taps[row], slab, preferred_element_type=F32).astype(BF16)
        spread[:, row] = pulled.reshape(basis_count, cols, channels)
        return carry

    lax.fori_loop(0, rows, one_row, 0, unroll=16)
    total = None
    for basis in range(basis_count):
        part = lax.dot_general(
            spread[basis].reshape(rows * cols, channels),
            mixing[basis],
            (((1,), (1,)), ((), ())),
            preferred_element_type=F32,
        )
        total = part if total is None else total + part
    out[...] = total.reshape(rows, cols, channels).astype(BF16)


def pair_sum_kernel(after, ready_w, ready_e, keep, recv, out):
    out[...] = (keep[...] + recv[...].astype(F32)).astype(BF16)


def chip_sum_kernel(after, parts, out):
    total = parts[0].astype(F32)
    for chip in range(1, parts.shape[0]):
        total = total + parts[chip].astype(F32)
    out[...] = total.astype(BF16)


def four_sum_kernel(one, two, three, four, out):
    near = one[...].astype(F32) + two[...].astype(F32)
    far = three[...].astype(F32) + four[...].astype(F32)
    out[...] = (near + far).astype(BF16)


def last_sum_kernel(normalizer, place, own, by_z, by_x, by_both, out):
    low = lax.rem(place[2], 2)
    shape = (2,) + out.shape[1:]
    mine = own[...].astype(F32) + by_z[...].astype(F32)
    other = by_x[...].astype(F32) + by_both[...].astype(F32)
    out[pl.ds(2 * low, 2)] = (mine * normalizer).reshape(shape)
    out[pl.ds(2 * (1 - low), 2)] = (other * normalizer).reshape(shape)


LAT = ("y", "xh", "core")
LON = ("xl", "z")
CROSS = ("xh", "xl")


def shift(cells, axis, count, step):
    return lax.ppermute(cells, axis, [(i, (i + step) % count) for i in range(count)])


def swap(cells, axis, count, mask):
    return lax.ppermute(cells, axis, [(i, i ^ mask) for i in range(count)])


def call(kernel, outs, args, specs, name, scratch=(), flops=0, moved=0):
    return pl.pallas_call(
        kernel,
        out_shape=outs,
        in_specs=specs,
        out_specs=jax.tree.map(lambda _: VMEM, outs),
        scratch_shapes=list(scratch),
        compiler_params=PARAMS,
        cost_estimate=pl.CostEstimate(flops=flops, bytes_accessed=moved, transcendentals=0),
        name=name,
    )(*args)


def shaped(shape, dtype):
    return jax.ShapeDtypeStruct(shape, dtype)


def local(field, filter_values, block_lat, block_lon, mixing, cotangent):
    rows, cols, channels = field.shape
    basis_count, _, blocks, taps = filter_values.shape
    lats = lax.axis_size(LAT)
    lons = lax.axis_size(LON)
    place = jnp.stack(
        [
            lax.axis_index(LAT) * rows,
            lax.axis_index("y"),
            lax.axis_index(CROSS),
            lax.axis_index("core"),
            lax.axis_index("z"),
            jnp.int32(rows * lats),
        ]
    ).astype(jnp.int32)
    both = (field, cotangent)
    odd = lax.axis_index("core") == 1
    top = jnp.stack([cells[:HL] for cells in both])
    bottom = jnp.stack([cells[rows - HL :] for cells in both])
    inner = jnp.where(odd, top, bottom)
    outer = jnp.where(odd, bottom, top)
    west = shift(field[:, cols - WL :], LON, lons, 1)
    east = shift(field[:, :WL], LON, lons, -1)
    psi = filter_values.transpose(0, 2, 3, 1)
    lat = block_lat.T
    lon = block_lon.T
    wide = cols + 2 * WL
    lines = basis_count * blocks * (taps + 2)
    fwd_taps = call(
        forward_taps_kernel,
        shaped((rows, basis_count * cols, blocks * wide), BF16),
        (place, psi, lat, lon),
        [SMEM] + [VMEM] * 3,
        "forward_taps",
        [pltpu.VMEM((lines, 128), BF16), pltpu.VMEM((lines, 128), F32)],
        flops=1_000_000_000,
        moved=1_000_000,
    )
    inner = swap(inner, LAT, lats, 1)
    pairs = [(0, 0), (lats - 1, lats - 1)]
    for low in range(1, lats - 1, 2):
        pairs += [(low, low + 1), (low + 1, low)]
    outer = lax.ppermute(outer, LAT, pairs)
    rim = shaped((2, 2, HL, WL, channels), BF16)
    side = shaped((rows, WL, channels), BF16)
    rim_to_east, rim_to_west, cot_to_east, cot_to_west = call(
        rims_kernel,
        (rim, rim, side, side),
        (place, fwd_taps, inner, outer, cotangent),
        [SMEM] + [VMEM] * 4,
        "rims",
        moved=1_000_000,
    )
    rims_w = shift(rim_to_east, LON, lons, 1)
    rims_e = shift(rim_to_west, LON, lons, -1)
    share = basis_count * channels // lats
    keep, send, filtered = call(
        filter_kernel,
        (
            shaped((lats, share // 2, channels), F32),
            shaped((lats, share // 2, channels), BF16),
            shaped((basis_count, rows, cols, channels), BF16),
        ),
        (place, lat, fwd_taps, field, west, east, inner, outer, rims_w, rims_e, cotangent),
        [SMEM] * 2 + [VMEM] * 9,
        "filtering",
        [pltpu.VMEM((rows + 2 * HL, wide, channels), BF16)],
        flops=FILTER_COST,
        moved=8_000_000,
    )
    recv = swap(send, "core", 2, 1)
    cot_west = shift(cot_to_east, LON, lons, 1)
    cot_east = shift(cot_to_west, LON, lons, -1)
    token = shaped((8, 128), F32)
    output, token_one = call(
        output_kernel,
        (shaped((rows, cols, channels), BF16), token),
        (filtered, mixing),
        [VMEM] * 2,
        "mixed",
        flops=MIXED_COST,
        moved=4_500_000,
    )
    summed = call(
        pair_sum_kernel,
        shaped(keep.shape, BF16),
        (token_one, cot_west, cot_east, keep, recv),
        [VMEM] * 5,
        "pair_sum",
        flops=keep.size,
        moved=keep.size * 8,
    )
    parts = lax.all_to_all(summed, ("y", "xh", "xl"), 0, 0)

    adj_taps = call(
        adjoint_taps_kernel,
        shaped((rows, basis_count * cols, SPAN * wide), BF16),
        (place, summed, psi, lat, lon),
        [SMEM] + [VMEM] * 4,
        "adjoint_taps",
        [
            pltpu.VMEM((lines, 128), BF16),
            pltpu.VMEM((lines, -(-SPAN * wide // 128) * 128), F32),
        ],
        flops=2_000_000_000,
        moved=2_000_000,
    )
    field_grad, token_two = call(
        adjoint_kernel,
        (shaped((rows, cols, channels), BF16), token),
        (
            place,
            summed,
            adj_taps,
            cotangent,
            cot_west,
            cot_east,
            inner,
            outer,
            rims_w,
            rims_e,
            mixing,
        ),
        [SMEM, VMEM] + [VMEM] * 9,
        "adjoint",
        [
            pltpu.VMEM((rows + 2 * HL, wide, channels), BF16),
            pltpu.VMEM((basis_count, rows, cols, channels), BF16),
        ],
        flops=3_000_000_000,
        moved=6_000_000,
    )

    _, deep, _ = parts.shape
    part = call(
        chip_sum_kernel,
        shaped((deep, channels), BF16),
        (token_two, parts),
        [VMEM] * 2,
        "chip_sum",
        flops=parts.size,
        moved=parts.size * 2,
    )
    part = call(
        four_sum_kernel,
        shaped((deep, channels), BF16),
        (part, *(swap(part, "z", 8, mask) for mask in (2, 4, 6))),
        [VMEM] * 4,
        "four_sum",
        flops=part.size * 4,
        moved=part.size * 10,
    )
    normalizer = 1.0 / math.sqrt(rows * lats * cols * lons)
    mixing_grad = call(
        functools.partial(last_sum_kernel, normalizer),
        shaped((basis_count, channels // lats, channels), F32),
        (place, part, swap(part, "z", 8, 1), swap(part, "xl", 2, 1), swap(part, LON, 16, 9)),
        [SMEM] + [VMEM] * 4,
        "last_sum",
        flops=part.size * 4,
        moved=part.size * 16,
    )
    return (output, field_grad, mixing_grad)


def solution(mesh):
    grid = Mesh(mesh.devices.reshape(4, 2, 2, 2, 8), ("y", "xh", "core", "xl", "z"))
    return jax.shard_map(
        local,
        mesh=grid,
        in_specs=(P(LAT, LON, None), P(), P(), P(), P(), P(LAT, LON, None)),
        out_specs=(P(LAT, LON, None), P(LAT, LON, None), P(None, LAT, None)),
        check_vma=False,
    )
```

```python
import functools
import math

import jax
import jax.numpy as jnp
from jax import lax
from jax.experimental import pallas as pl
from jax.experimental.pallas import tpu as pltpu
from jax.sharding import Mesh
from jax.sharding import PartitionSpec as P

HL = 2
MIXED_COST = 60_000_000_000
FILTER_COST = 20_000_000_000
WL = 16
SPAN = 2 * HL + 1
F32 = jnp.float32
BF16 = jnp.bfloat16
VMEM = pl.BlockSpec(memory_space=pltpu.VMEM)
SMEM = pl.BlockSpec(memory_space=pltpu.SMEM)
PARAMS = pltpu.CompilerParams(vmem_limit_bytes=24 * 1024 * 1024)


def iota(shape, axis):
    return lax.broadcasted_iota(jnp.int32, shape, axis)


def placed_lines(weights, distance, count):
    kinds = iota((weights.shape[0], 1), 0) % count
    return jnp.where(distance == kinds, weights, 0.0)


def store_bands(out, row, lines, basis_count, count, taps):
    cols = out.shape[1] // basis_count
    width = out.shape[2]
    for basis in range(basis_count):
        first = basis * count
        line = lines[first : first + 1]
        for tap in range(1, taps):
            line = line + lines[first + tap : first + tap + 1]
        for lane in range(0, width, 128):
            tile = jnp.broadcast_to(line[:, lane : lane + 128], (cols, 128))
            tile = pltpu.roll(tile, 0, 1, stride=1, stride_axis=0).astype(BF16)
            room = min(128, width - lane)
            out[row, basis * cols : (basis + 1) * cols, lane : lane + room] = tile[:, :room]


def gathered(near_all, place, psi, lat, lon, rows):
    basis_count, blocks, taps, cycles = psi.shape
    lines = basis_count * (taps + 2)
    cycle = iota((cycles, 128), 0) - place[0] + HL
    hot = ((iota((cycles, 128), 1) == cycle) & (cycle < rows + 2 * HL)).astype(BF16)
    for block in range(blocks):
        turns = [lon[block : block + 1].astype(F32), lat[block : block + 1].astype(F32)]
        here = []
        for basis in range(basis_count):
            here += [psi[basis, block].astype(F32)] + turns
        here = jnp.concatenate(here, axis=0).astype(BF16)
        near_all[block * lines : (block + 1) * lines] = jnp.dot(
            here, hot, preferred_element_type=F32
        ).astype(BF16)


def forward_taps_kernel(place, psi, lat, lon, forward, near_all, spread):
    rows = forward.shape[0] - 2 * HL
    basis_count, blocks, taps, cycles = psi.shape
    count = taps + 2
    wide = forward.shape[2] // blocks
    lines = basis_count * count
    gathered(near_all, place, psi, lat, lon, rows)
    near = near_all[...]
    slot = iota((128, 128), 0)
    base = iota((1, wide), 1) - WL

    def one_row(row, carry):
        weights_all = jnp.dot(near, (slot == row).astype(BF16), preferred_element_type=F32)
        totals = []
        for block in range(blocks):
            weights = weights_all[block * lines : (block + 1) * lines, :wide]
            distance = base - weights[taps : taps + 1].astype(jnp.int32)
            totals.append(placed_lines(weights, distance, count))
        store_bands(forward, row, jnp.concatenate(totals, axis=1), basis_count, count, taps)
        return carry

    lax.fori_loop(0, rows + 2 * HL, one_row, 0, unroll=20)


def adjoint_taps_kernel(place, after, psi, lat, lon, adjoint, near_all, adj_wide):
    rows = adjoint.shape[0]
    basis_count, blocks, taps, cycles = psi.shape
    count = taps + 2
    wide = adjoint.shape[2] // SPAN
    lines = basis_count * count
    gathered(near_all, place, psi, lat, lon, rows)
    near = near_all[...]
    lanes = adj_wide.shape[1]
    slot = iota((128, lanes), 0) - iota((128, lanes), 1) // wide
    inside = iota((128, lanes), 1) // wide < SPAN
    turn = iota((1, lanes), 1)
    wanted = HL - turn // wide
    base = WL - turn % wide

    def one_row(row, carry):
        adj_wide[...] = jnp.dot(
            near, ((slot == row) & inside).astype(BF16), preferred_element_type=F32
        )
        total = None
        for block in range(blocks):
            weights = adj_wide[block * lines : (block + 1) * lines, :]
            shift = weights[taps : taps + 1].astype(jnp.int32)
            match = weights[taps + 1 : taps + 2].astype(jnp.int32) == wanted
            value = placed_lines(weights, base - jnp.where(match, shift, 4 * wide), count)
            total = value if total is None else total + value
        store_bands(adjoint, row, total, basis_count, count, taps)
        return carry

    lax.fori_loop(0, rows, one_row, 0, unroll=4)


def rims_kernel(place, inner, outer, to_east, to_west):
    cols = inner.shape[2]
    odd = place[3] == 1
    north = jnp.where(odd, inner[...], outer[...])
    south = jnp.where(odd, outer[...], inner[...])
    to_east[0] = north[:, :, cols - WL :]
    to_east[1] = south[:, :, cols - WL :]
    to_west[0] = north[:, :, :WL]
    to_west[1] = south[:, :, :WL]


def assemble(which, place, extended, center, west, east, inner, outer, rims_w, rims_e):
    rows, cols, _ = center.shape
    extended[HL : HL + rows, 0:WL] = west[...]
    extended[HL : HL + rows, WL : WL + cols] = center[...]
    extended[HL : HL + rows, WL + cols :] = east[...]
    odd = place[3] == 1
    above = place[0] > 0
    below = place[0] + rows < place[5]
    none = jnp.zeros((), BF16)
    north = jnp.where(odd, inner[which], outer[which])
    south = jnp.where(odd, outer[which], inner[which])
    for side, (inside, rim, lines) in enumerate(
        ((above, north, slice(0, HL)), (below, south, slice(HL + rows, None)))
    ):
        extended[lines, 0:WL] = jnp.where(inside, rims_w[side, which], none)
        extended[lines, WL : WL + cols] = jnp.where(inside, rim, none)
        extended[lines, WL + cols :] = jnp.where(inside, rims_e[side, which], none)


def terms_kernel(
    place, lat, taps, center, west, east, cot, inner, outer, keep, send, extended, filtered, around
):
    rows, cols, channels = center.shape
    basis_count = filtered.shape[0]
    blocks = lat.shape[0]
    wide_rows = rows + 2 * HL
    extended[0:rows, 0:WL] = west[...]
    extended[0:rows, WL : WL + cols] = center[...]
    extended[0:rows, WL + cols :] = east[...]
    extended[rows] = jnp.zeros(extended.shape[1:], BF16)
    odd = place[3] == 1
    around[0:HL] = jnp.where(odd, inner[1], outer[1])
    around[HL : HL + rows] = cot[...]
    around[HL + rows :] = jnp.where(odd, outer[1], inner[1])

    def one_row(row, carry):
        cycle = jnp.clip(place[0] + row - HL, 0, place[5] - 1)
        slabs = []
        for block in range(blocks):
            source = row - HL + lat[block, cycle]
            inside = (source >= 0) & (source < rows)
            slabs.append(extended[jnp.where(inside, source, rows)])
        slab = jnp.concatenate(slabs, axis=0)
        part = jnp.dot(taps[row], slab, preferred_element_type=F32).astype(BF16)
        filtered[:, row] = part.reshape(basis_count, cols, channels)
        return carry

    lax.fori_loop(0, wide_rows, one_row, 0, unroll=20)
    cot_flat = around[...].reshape(wide_rows * cols, channels)
    pairs = keep.shape[0] // 2
    share = channels // (2 * pairs)
    per = keep.shape[1] // share
    core = place[3]
    for basis in range(basis_count):
        terms = lax.dot_general(
            filtered[basis].reshape(wide_rows * cols, channels),
            cot_flat,
            (((0,), (0,)), ((), ())),
            preferred_element_type=F32,
        ).reshape(pairs, 2, share, channels)
        lines = slice(basis % per * share, (basis % per + 1) * share)
        mine = jnp.where(core == 0, terms[:, 0], terms[:, 1])
        other = jnp.where(core == 0, terms[:, 1], terms[:, 0]).astype(BF16)
        for pair in range(pairs):
            keep[2 * pair + basis // per, lines] = mine[pair]
            send[2 * pair + basis // per, lines] = other[pair]


def ready_kernel(west, east, token):
    token[...] = jnp.zeros_like(token)


def output_kernel(
    place, after, lat, taps, center, west, east, inner, outer, rims_w, rims_e, mixing, out, token, extended, filtered
):
    token[...] = jnp.zeros_like(token)
    rows, cols, channels = center.shape
    basis_count = mixing.shape[0]
    blocks = lat.shape[0]
    assemble(0, place, extended, center, west, east, inner, outer, rims_w, rims_e)

    def one_row(row, carry):
        slabs = [extended[row + HL + lat[block, place[0] + row]] for block in range(blocks)]
        slab = jnp.concatenate(slabs, axis=0)
        part = jnp.dot(taps[row + HL], slab, preferred_element_type=F32).astype(BF16)
        filtered[:, row] = part.reshape(basis_count, cols, channels)
        return carry

    lax.fori_loop(0, rows, one_row, 0, unroll=16)
    total = None
    for basis in range(basis_count):
        part = jnp.dot(
            filtered[basis].reshape(rows * cols, channels),
            mixing[basis],
            preferred_element_type=F32,
        )
        total = part if total is None else total + part
    out[...] = total.reshape(rows, cols, channels).astype(BF16)


def adjoint_kernel(
    place, after, taps, center, west, east, inner, outer, rims_w, rims_e, mixing, out, token, extended, spread
):
    token[...] = jnp.zeros_like(token)
    rows, cols, channels = center.shape
    basis_count = mixing.shape[0]
    assemble(1, place, extended, center, west, east, inner, outer, rims_w, rims_e)

    def one_row(row, carry):
        slab = extended[pl.ds(row, SPAN)].reshape(SPAN * (cols + 2 * WL), channels)
        pulled = jnp.dot(taps[row], slab, preferred_element_type=F32).astype(BF16)
        spread[:, row] = pulled.reshape(basis_count, cols, channels)
        return carry

    lax.fori_loop(0, rows, one_row, 0, unroll=16)
    total = None
    for basis in range(basis_count):
        part = lax.dot_general(
            spread[basis].reshape(rows * cols, channels),
            mixing[basis],
            (((1,), (1,)), ((), ())),
            preferred_element_type=F32,
        )
        total = part if total is None else total + part
    out[...] = total.reshape(rows, cols, channels).astype(BF16)


def pair_sum_kernel(after, keep, recv, out):
    out[...] = (keep[...] + recv[...].astype(F32)).astype(BF16)


def chip_sum_kernel(after_one, after_two, parts, out):
    total = parts[0].astype(F32)
    for chip in range(1, parts.shape[0]):
        total = total + parts[chip].astype(F32)
    out[...] = total.astype(BF16)


def four_sum_kernel(one, two, three, four, out):
    near = one[...].astype(F32) + two[...].astype(F32)
    far = three[...].astype(F32) + four[...].astype(F32)
    out[...] = (near + far).astype(BF16)


def last_sum_kernel(normalizer, place, own, by_z, by_x, by_both, out):
    low = lax.rem(place[2], 2)
    shape = (2,) + out.shape[1:]
    mine = own[...].astype(F32) + by_z[...].astype(F32)
    other = by_x[...].astype(F32) + by_both[...].astype(F32)
    out[pl.ds(2 * low, 2)] = (mine * normalizer).reshape(shape)
    out[pl.ds(2 * (1 - low), 2)] = (other * normalizer).reshape(shape)


LAT = ("y", "xh", "core")
LON = ("xl", "z")
CROSS = ("xh", "xl")


def shift(cells, axis, count, step):
    return lax.ppermute(cells, axis, [(i, (i + step) % count) for i in range(count)])


def swap(cells, axis, count, mask):
    return lax.ppermute(cells, axis, [(i, i ^ mask) for i in range(count)])


def call(kernel, outs, args, specs, name, scratch=(), flops=0, moved=0):
    return pl.pallas_call(
        kernel,
        out_shape=outs,
        in_specs=specs,
        out_specs=jax.tree.map(lambda _: VMEM, outs),
        scratch_shapes=list(scratch),
        compiler_params=PARAMS,
        cost_estimate=pl.CostEstimate(flops=flops, bytes_accessed=moved, transcendentals=0),
        name=name,
    )(*args)


def shaped(shape, dtype):
    return jax.ShapeDtypeStruct(shape, dtype)


def local(field, filter_values, block_lat, block_lon, mixing, cotangent):
    rows, cols, channels = field.shape
    basis_count, _, blocks, taps = filter_values.shape
    lats = lax.axis_size(LAT)
    lons = lax.axis_size(LON)
    place = jnp.stack(
        [
            lax.axis_index(LAT) * rows,
            lax.axis_index("y"),
            lax.axis_index(CROSS),
            lax.axis_index("core"),
            lax.axis_index("z"),
            jnp.int32(rows * lats),
        ]
    ).astype(jnp.int32)
    both = (field, cotangent)
    odd = lax.axis_index("core") == 1
    top = jnp.stack([cells[:HL] for cells in both])
    bottom = jnp.stack([cells[rows - HL :] for cells in both])
    inner = jnp.where(odd, top, bottom)
    outer = jnp.where(odd, bottom, top)
    west = shift(field[:, cols - WL :], LON, lons, 1)
    east = shift(field[:, :WL], LON, lons, -1)
    psi = filter_values.transpose(0, 2, 3, 1)
    lat = block_lat.T
    lon = block_lon.T
    wide = cols + 2 * WL
    lines = basis_count * blocks * (taps + 2)
    fwd_taps = call(
        forward_taps_kernel,
        shaped((rows + 2 * HL, basis_count * cols, blocks * wide), BF16),
        (place, psi, lat, lon),
        [SMEM] + [VMEM] * 3,
        "forward_taps",
        [pltpu.VMEM((lines, 128), BF16), pltpu.VMEM((lines, 128), F32)],
        flops=1_000_000_000,
        moved=1_000_000,
    )
    inner = swap(inner, LAT, lats, 1)
    pairs = [(0, 0), (lats - 1, lats - 1)]
    for low in range(1, lats - 1, 2):
        pairs += [(low, low + 1), (low + 1, low)]
    outer = lax.ppermute(outer, LAT, pairs)
    rim = shaped((2, 2, HL, WL, channels), BF16)
    rim_to_east, rim_to_west = call(
        rims_kernel, (rim, rim), (place, inner, outer), [SMEM] + [VMEM] * 2, "rims", moved=1_000_000
    )
    rims_w = shift(rim_to_east, LON, lons, 1)
    rims_e = shift(rim_to_west, LON, lons, -1)
    share = basis_count * channels // lats
    keep, send = call(
        terms_kernel,
        (
            shaped((lats, share // 2, channels), F32),
            shaped((lats, share // 2, channels), BF16),
        ),
        (place, lat, fwd_taps, field, west, east, cotangent, inner, outer),
        [SMEM] * 2 + [VMEM] * 7,
        "terms",
        [
            pltpu.VMEM((rows + 1, wide, channels), BF16),
            pltpu.VMEM((basis_count, rows + 2 * HL, cols, channels), BF16),
            pltpu.VMEM((rows + 2 * HL, cols, channels), BF16),
        ],
        flops=FILTER_COST,
        moved=8_000_000,
    )
    recv = swap(send, "core", 2, 1)
    cot_west = shift(cotangent[:, cols - WL :], LON, lons, 1)
    cot_east = shift(cotangent[:, :WL], LON, lons, -1)
    token = shaped((8, 128), F32)
    ready = call(
        ready_kernel,
        token,
        (cot_west, cot_east),
        [VMEM] * 2,
        "ready",
        flops=MIXED_COST,
        moved=1_000_000,
    )
    summed = call(
        pair_sum_kernel,
        shaped(keep.shape, BF16),
        (ready, keep, recv),
        [VMEM] * 3,
        "pair_sum",
        flops=keep.size,
        moved=keep.size * 8,
    )
    parts = lax.all_to_all(summed, ("y", "xh", "xl"), 0, 0)

    output, token_one = call(
        output_kernel,
        (shaped((rows, cols, channels), BF16), token),
        (
            place,
            summed,
            lat,
            fwd_taps,
            field,
            west,
            east,
            inner,
            outer,
            rims_w,
            rims_e,
            mixing,
        ),
        [SMEM, VMEM, SMEM] + [VMEM] * 9,
        "output",
        [
            pltpu.VMEM((rows + 2 * HL, wide, channels), BF16),
            pltpu.VMEM((basis_count, rows, cols, channels), BF16),
        ],
        flops=3_000_000_000,
        moved=6_000_000,
    )
    adj_taps = call(
        adjoint_taps_kernel,
        shaped((rows, basis_count * cols, SPAN * wide), BF16),
        (place, summed, psi, lat, lon),
        [SMEM] + [VMEM] * 4,
        "adjoint_taps",
        [
            pltpu.VMEM((lines, 128), BF16),
            pltpu.VMEM((lines, -(-SPAN * wide // 128) * 128), F32),
        ],
        flops=2_000_000_000,
        moved=2_000_000,
    )
    field_grad, token_two = call(
        adjoint_kernel,
        (shaped((rows, cols, channels), BF16), token),
        (
            place,
            summed,
            adj_taps,
            cotangent,
            cot_west,
            cot_east,
            inner,
            outer,
            rims_w,
            rims_e,
            mixing,
        ),
        [SMEM, VMEM] + [VMEM] * 9,
        "adjoint",
        [
            pltpu.VMEM((rows + 2 * HL, wide, channels), BF16),
            pltpu.VMEM((basis_count, rows, cols, channels), BF16),
        ],
        flops=3_000_000_000,
        moved=6_000_000,
    )

    _, deep, _ = parts.shape
    part = call(
        chip_sum_kernel,
        shaped((deep, channels), BF16),
        (token_one, token_two, parts),
        [VMEM] * 3,
        "chip_sum",
        flops=parts.size,
        moved=parts.size * 2,
    )
    part = call(
        four_sum_kernel,
        shaped((deep, channels), BF16),
        (part, *(swap(part, "z", 8, mask) for mask in (2, 4, 6))),
        [VMEM] * 4,
        "four_sum",
        flops=part.size * 4,
        moved=part.size * 10,
    )
    normalizer = 1.0 / math.sqrt(rows * lats * cols * lons)
    mixing_grad = call(
        functools.partial(last_sum_kernel, normalizer),
        shaped((basis_count, channels // lats, channels), F32),
        (place, part, swap(part, "z", 8, 1), swap(part, "xl", 2, 1), swap(part, LON, 16, 9)),
        [SMEM] + [VMEM] * 4,
        "last_sum",
        flops=part.size * 4,
        moved=part.size * 16,
    )
    return (output, field_grad, mixing_grad)


def solution(mesh):
    grid = Mesh(mesh.devices.reshape(4, 2, 2, 2, 8), ("y", "xh", "core", "xl", "z"))
    return jax.shard_map(
        local,
        mesh=grid,
        in_specs=(P(LAT, LON, None), P(), P(), P(), P(), P(LAT, LON, None)),
        out_specs=(P(LAT, LON, None), P(LAT, LON, None), P(None, LAT, None)),
        check_vma=False,
    )
```

```python
import functools
import math

import jax
import jax.numpy as jnp
from jax import lax
from jax.experimental import pallas as pl
from jax.experimental.pallas import tpu as pltpu
from jax.sharding import Mesh
from jax.sharding import PartitionSpec as P

HL = 2
MIXED_COST = 60_000_000_000
FILTER_COST = 20_000_000_000
WL = 16
SPAN = 2 * HL + 1
F32 = jnp.float32
BF16 = jnp.bfloat16
VMEM = pl.BlockSpec(memory_space=pltpu.VMEM)
SMEM = pl.BlockSpec(memory_space=pltpu.SMEM)
PARAMS = pltpu.CompilerParams(vmem_limit_bytes=24 * 1024 * 1024)


def iota(shape, axis):
    return lax.broadcasted_iota(jnp.int32, shape, axis)


def placed_lines(weights, distance, count):
    kinds = iota((weights.shape[0], 1), 0) % count
    return jnp.where(distance == kinds, weights, 0.0)


def store_bands(out, row, lines, basis_count, count, taps):
    cols = out.shape[1] // basis_count
    width = out.shape[2]
    for basis in range(basis_count):
        first = basis * count
        line = lines[first : first + 1]
        for tap in range(1, taps):
            line = line + lines[first + tap : first + tap + 1]
        for lane in range(0, width, 128):
            tile = jnp.broadcast_to(line[:, lane : lane + 128], (cols, 128))
            tile = pltpu.roll(tile, 0, 1, stride=1, stride_axis=0).astype(BF16)
            room = min(128, width - lane)
            out[row, basis * cols : (basis + 1) * cols, lane : lane + room] = tile[:, :room]


def gathered(near_all, place, psi, lat, lon, rows):
    basis_count, blocks, taps, cycles = psi.shape
    lines = basis_count * (taps + 2)
    cycle = iota((cycles, 128), 0) - place[0] + HL
    hot = ((iota((cycles, 128), 1) == cycle) & (cycle < rows + 2 * HL)).astype(BF16)
    for block in range(blocks):
        turns = [lon[block : block + 1].astype(F32), lat[block : block + 1].astype(F32)]
        here = []
        for basis in range(basis_count):
            here += [psi[basis, block].astype(F32)] + turns
        here = jnp.concatenate(here, axis=0).astype(BF16)
        near_all[block * lines : (block + 1) * lines] = jnp.dot(
            here, hot, preferred_element_type=F32
        ).astype(BF16)


def forward_taps_kernel(place, psi, lat, lon, forward, near_all, spread):
    rows = forward.shape[0] - 2 * HL
    basis_count, blocks, taps, cycles = psi.shape
    count = taps + 2
    wide = forward.shape[2] // blocks
    lines = basis_count * count
    gathered(near_all, place, psi, lat, lon, rows)
    near = near_all[...]
    slot = iota((128, 128), 0)
    base = iota((1, wide), 1) - WL

    def one_row(row, carry):
        weights_all = jnp.dot(near, (slot == row).astype(BF16), preferred_element_type=F32)
        totals = []
        for block in range(blocks):
            weights = weights_all[block * lines : (block + 1) * lines, :wide]
            distance = base - weights[taps : taps + 1].astype(jnp.int32)
            totals.append(placed_lines(weights, distance, count))
        store_bands(forward, row, jnp.concatenate(totals, axis=1), basis_count, count, taps)
        return carry

    lax.fori_loop(0, rows + 2 * HL, one_row, 0, unroll=20)


def adjoint_taps_kernel(place, after, psi, lat, lon, adjoint, near_all, adj_wide):
    rows = adjoint.shape[0]
    basis_count, blocks, taps, cycles = psi.shape
    count = taps + 2
    wide = adjoint.shape[2] // SPAN
    lines = basis_count * count
    gathered(near_all, place, psi, lat, lon, rows)
    near = near_all[...]
    lanes = adj_wide.shape[1]
    slot = iota((128, lanes), 0) - iota((128, lanes), 1) // wide
    inside = iota((128, lanes), 1) // wide < SPAN
    turn = iota((1, lanes), 1)
    wanted = HL - turn // wide
    base = WL - turn % wide

    def one_row(row, carry):
        adj_wide[...] = jnp.dot(
            near, ((slot == row) & inside).astype(BF16), preferred_element_type=F32
        )
        total = None
        for block in range(blocks):
            weights = adj_wide[block * lines : (block + 1) * lines, :]
            shift = weights[taps : taps + 1].astype(jnp.int32)
            match = weights[taps + 1 : taps + 2].astype(jnp.int32) == wanted
            value = placed_lines(weights, base - jnp.where(match, shift, 4 * wide), count)
            total = value if total is None else total + value
        store_bands(adjoint, row, total, basis_count, count, taps)
        return carry

    lax.fori_loop(0, rows, one_row, 0, unroll=16)


def rims_kernel(place, inner, outer, to_east, to_west):
    cols = inner.shape[2]
    odd = place[3] == 1
    north = jnp.where(odd, inner[...], outer[...])
    south = jnp.where(odd, outer[...], inner[...])
    to_east[0] = north[:, :, cols - WL :]
    to_east[1] = south[:, :, cols - WL :]
    to_west[0] = north[:, :, :WL]
    to_west[1] = south[:, :, :WL]


def assemble(which, place, extended, center, west, east, inner, outer, rims_w, rims_e):
    rows, cols, _ = center.shape
    extended[HL : HL + rows, 0:WL] = west[...]
    extended[HL : HL + rows, WL : WL + cols] = center[...]
    extended[HL : HL + rows, WL + cols :] = east[...]
    odd = place[3] == 1
    above = place[0] > 0
    below = place[0] + rows < place[5]
    none = jnp.zeros((), BF16)
    north = jnp.where(odd, inner[which], outer[which])
    south = jnp.where(odd, outer[which], inner[which])
    for side, (inside, rim, lines) in enumerate(
        ((above, north, slice(0, HL)), (below, south, slice(HL + rows, None)))
    ):
        extended[lines, 0:WL] = jnp.where(inside, rims_w[side, which], none)
        extended[lines, WL : WL + cols] = jnp.where(inside, rim, none)
        extended[lines, WL + cols :] = jnp.where(inside, rims_e[side, which], none)


def terms_kernel(
    place, lat, taps, center, west, east, cot, inner, outer, keep, send, extended, filtered, around
):
    rows, cols, channels = center.shape
    basis_count = filtered.shape[0]
    blocks = lat.shape[0]
    wide_rows = rows + 2 * HL
    extended[0:rows, 0:WL] = west[...]
    extended[0:rows, WL : WL + cols] = center[...]
    extended[0:rows, WL + cols :] = east[...]
    extended[rows] = jnp.zeros(extended.shape[1:], BF16)
    odd = place[3] == 1
    around[0:HL] = jnp.where(odd, inner[1], outer[1])
    around[HL : HL + rows] = cot[...]
    around[HL + rows :] = jnp.where(odd, outer[1], inner[1])

    def one_row(row, carry):
        cycle = jnp.clip(place[0] + row - HL, 0, place[5] - 1)
        slabs = []
        for block in range(blocks):
            source = row - HL + lat[block, cycle]
            inside = (source >= 0) & (source < rows)
            slabs.append(extended[jnp.where(inside, source, rows)])
        slab = jnp.concatenate(slabs, axis=0)
        part = jnp.dot(taps[row], slab, preferred_element_type=F32).astype(BF16)
        filtered[:, row] = part.reshape(basis_count, cols, channels)
        return carry

    lax.fori_loop(0, wide_rows, one_row, 0, unroll=20)
    cot_flat = around[...].reshape(wide_rows * cols, channels)
    pairs = keep.shape[0] // 2
    share = channels // (2 * pairs)
    per = keep.shape[1] // share
    core = place[3]
    for basis in range(basis_count):
        terms = lax.dot_general(
            filtered[basis].reshape(wide_rows * cols, channels),
            cot_flat,
            (((0,), (0,)), ((), ())),
            preferred_element_type=F32,
        ).reshape(pairs, 2, share, channels)
        lines = slice(basis % per * share, (basis % per + 1) * share)
        mine = jnp.where(core == 0, terms[:, 0], terms[:, 1])
        other = jnp.where(core == 0, terms[:, 1], terms[:, 0]).astype(BF16)
        for pair in range(pairs):
            keep[2 * pair + basis // per, lines] = mine[pair]
            send[2 * pair + basis // per, lines] = other[pair]


def ready_kernel(west, east, token):
    token[...] = jnp.zeros_like(token)


def output_kernel(
    place, after, lat, taps, center, west, east, inner, outer, rims_w, rims_e, mixing, out, token, extended, filtered
):
    token[...] = jnp.zeros_like(token)
    rows, cols, channels = center.shape
    basis_count = mixing.shape[0]
    blocks = lat.shape[0]
    assemble(0, place, extended, center, west, east, inner, outer, rims_w, rims_e)

    def one_row(row, carry):
        slabs = [extended[row + HL + lat[block, place[0] + row]] for block in range(blocks)]
        slab = jnp.concatenate(slabs, axis=0)
        part = jnp.dot(taps[row + HL], slab, preferred_element_type=F32).astype(BF16)
        filtered[:, row] = part.reshape(basis_count, cols, channels)
        return carry

    lax.fori_loop(0, rows, one_row, 0, unroll=16)
    total = None
    for basis in range(basis_count):
        part = jnp.dot(
            filtered[basis].reshape(rows * cols, channels),
            mixing[basis],
            preferred_element_type=F32,
        )
        total = part if total is None else total + part
    out[...] = total.reshape(rows, cols, channels).astype(BF16)


def adjoint_kernel(
    place, after, taps, center, west, east, inner, outer, rims_w, rims_e, mixing, out, token, extended, spread
):
    token[...] = jnp.zeros_like(token)
    rows, cols, channels = center.shape
    basis_count = mixing.shape[0]
    assemble(1, place, extended, center, west, east, inner, outer, rims_w, rims_e)

    def one_row(row, carry):
        slab = extended[pl.ds(row, SPAN)].reshape(SPAN * (cols + 2 * WL), channels)
        pulled = jnp.dot(taps[row], slab, preferred_element_type=F32).astype(BF16)
        spread[:, row] = pulled.reshape(basis_count, cols, channels)
        return carry

    lax.fori_loop(0, rows, one_row, 0, unroll=16)
    total = None
    for basis in range(basis_count):
        part = lax.dot_general(
            spread[basis].reshape(rows * cols, channels),
            mixing[basis],
            (((1,), (1,)), ((), ())),
            preferred_element_type=F32,
        )
        total = part if total is None else total + part
    out[...] = total.reshape(rows, cols, channels).astype(BF16)


def pair_sum_kernel(after, keep, recv, out):
    out[...] = (keep[...] + recv[...].astype(F32)).astype(BF16)


def chip_sum_kernel(after_one, after_two, parts, out):
    total = parts[0].astype(F32)
    for chip in range(1, parts.shape[0]):
        total = total + parts[chip].astype(F32)
    out[...] = total.astype(BF16)


def four_sum_kernel(one, two, three, four, out):
    near = one[...].astype(F32) + two[...].astype(F32)
    far = three[...].astype(F32) + four[...].astype(F32)
    out[...] = (near + far).astype(BF16)


def last_sum_kernel(normalizer, place, own, by_z, by_x, by_both, out):
    low = lax.rem(place[2], 2)
    shape = (2,) + out.shape[1:]
    mine = own[...].astype(F32) + by_z[...].astype(F32)
    other = by_x[...].astype(F32) + by_both[...].astype(F32)
    out[pl.ds(2 * low, 2)] = (mine * normalizer).reshape(shape)
    out[pl.ds(2 * (1 - low), 2)] = (other * normalizer).reshape(shape)


LAT = ("y", "xh", "core")
LON = ("xl", "z")
CROSS = ("xh", "xl")


def shift(cells, axis, count, step):
    return lax.ppermute(cells, axis, [(i, (i + step) % count) for i in range(count)])


def swap(cells, axis, count, mask):
    return lax.ppermute(cells, axis, [(i, i ^ mask) for i in range(count)])


def call(kernel, outs, args, specs, name, scratch=(), flops=0, moved=0):
    return pl.pallas_call(
        kernel,
        out_shape=outs,
        in_specs=specs,
        out_specs=jax.tree.map(lambda _: VMEM, outs),
        scratch_shapes=list(scratch),
        compiler_params=PARAMS,
        cost_estimate=pl.CostEstimate(flops=flops, bytes_accessed=moved, transcendentals=0),
        name=name,
    )(*args)


def shaped(shape, dtype):
    return jax.ShapeDtypeStruct(shape, dtype)


def local(field, filter_values, block_lat, block_lon, mixing, cotangent):
    rows, cols, channels = field.shape
    basis_count, _, blocks, taps = filter_values.shape
    lats = lax.axis_size(LAT)
    lons = lax.axis_size(LON)
    place = jnp.stack(
        [
            lax.axis_index(LAT) * rows,
            lax.axis_index("y"),
            lax.axis_index(CROSS),
            lax.axis_index("core"),
            lax.axis_index("z"),
            jnp.int32(rows * lats),
        ]
    ).astype(jnp.int32)
    both = (field, cotangent)
    odd = lax.axis_index("core") == 1
    top = jnp.stack([cells[:HL] for cells in both])
    bottom = jnp.stack([cells[rows - HL :] for cells in both])
    inner = jnp.where(odd, top, bottom)
    outer = jnp.where(odd, bottom, top)
    west = shift(field[:, cols - WL :], LON, lons, 1)
    east = shift(field[:, :WL], LON, lons, -1)
    psi = filter_values.transpose(0, 2, 3, 1)
    lat = block_lat.T
    lon = block_lon.T
    wide = cols + 2 * WL
    lines = basis_count * blocks * (taps + 2)
    fwd_taps = call(
        forward_taps_kernel,
        shaped((rows + 2 * HL, basis_count * cols, blocks * wide), BF16),
        (place, psi, lat, lon),
        [SMEM] + [VMEM] * 3,
        "forward_taps",
        [pltpu.VMEM((lines, 128), BF16), pltpu.VMEM((lines, 128), F32)],
        flops=1_000_000_000,
        moved=1_000_000,
    )
    inner = swap(inner, LAT, lats, 1)
    pairs = [(0, 0), (lats - 1, lats - 1)]
    for low in range(1, lats - 1, 2):
        pairs += [(low, low + 1), (low + 1, low)]
    outer = lax.ppermute(outer, LAT, pairs)
    rim = shaped((2, 2, HL, WL, channels), BF16)
    rim_to_east, rim_to_west = call(
        rims_kernel, (rim, rim), (place, inner, outer), [SMEM] + [VMEM] * 2, "rims", moved=1_000_000
    )
    rims_w = shift(rim_to_east, LON, lons, 1)
    rims_e = shift(rim_to_west, LON, lons, -1)
    share = basis_count * channels // lats
    keep, send = call(
        terms_kernel,
        (
            shaped((lats, share // 2, channels), F32),
            shaped((lats, share // 2, channels), BF16),
        ),
        (place, lat, fwd_taps, field, west, east, cotangent, inner, outer),
        [SMEM] * 2 + [VMEM] * 7,
        "terms",
        [
            pltpu.VMEM((rows + 1, wide, channels), BF16),
            pltpu.VMEM((basis_count, rows + 2 * HL, cols, channels), BF16),
            pltpu.VMEM((rows + 2 * HL, cols, channels), BF16),
        ],
        flops=FILTER_COST,
        moved=8_000_000,
    )
    recv = swap(send, "core", 2, 1)
    cot_west = shift(cotangent[:, cols - WL :], LON, lons, 1)
    cot_east = shift(cotangent[:, :WL], LON, lons, -1)
    token = shaped((8, 128), F32)
    ready = call(
        ready_kernel,
        token,
        (cot_west, cot_east),
        [VMEM] * 2,
        "ready",
        flops=MIXED_COST,
        moved=1_000_000,
    )
    summed = call(
        pair_sum_kernel,
        shaped(keep.shape, BF16),
        (ready, keep, recv),
        [VMEM] * 3,
        "pair_sum",
        flops=keep.size,
        moved=keep.size * 8,
    )
    parts = lax.all_to_all(summed, ("y", "xh", "xl"), 0, 0)

    output, token_one = call(
        output_kernel,
        (shaped((rows, cols, channels), BF16), token),
        (
            place,
            summed,
            lat,
            fwd_taps,
            field,
            west,
            east,
            inner,
            outer,
            rims_w,
            rims_e,
            mixing,
        ),
        [SMEM, VMEM, SMEM] + [VMEM] * 9,
        "output",
        [
            pltpu.VMEM((rows + 2 * HL, wide, channels), BF16),
            pltpu.VMEM((basis_count, rows, cols, channels), BF16),
        ],
        flops=3_000_000_000,
        moved=6_000_000,
    )
    adj_taps = call(
        adjoint_taps_kernel,
        shaped((rows, basis_count * cols, SPAN * wide), BF16),
        (place, summed, psi, lat, lon),
        [SMEM] + [VMEM] * 4,
        "adjoint_taps",
        [
            pltpu.VMEM((lines, 128), BF16),
            pltpu.VMEM((lines, -(-SPAN * wide // 128) * 128), F32),
        ],
        flops=2_000_000_000,
        moved=2_000_000,
    )
    field_grad, token_two = call(
        adjoint_kernel,
        (shaped((rows, cols, channels), BF16), token),
        (
            place,
            summed,
            adj_taps,
            cotangent,
            cot_west,
            cot_east,
            inner,
            outer,
            rims_w,
            rims_e,
            mixing,
        ),
        [SMEM, VMEM] + [VMEM] * 9,
        "adjoint",
        [
            pltpu.VMEM((rows + 2 * HL, wide, channels), BF16),
            pltpu.VMEM((basis_count, rows, cols, channels), BF16),
        ],
        flops=3_000_000_000,
        moved=6_000_000,
    )

    _, deep, _ = parts.shape
    part = call(
        chip_sum_kernel,
        shaped((deep, channels), BF16),
        (token_one, token_two, parts),
        [VMEM] * 3,
        "chip_sum",
        flops=parts.size,
        moved=parts.size * 2,
    )
    part = call(
        four_sum_kernel,
        shaped((deep, channels), BF16),
        (part, *(swap(part, "z", 8, mask) for mask in (2, 4, 6))),
        [VMEM] * 4,
        "four_sum",
        flops=part.size * 4,
        moved=part.size * 10,
    )
    normalizer = 1.0 / math.sqrt(rows * lats * cols * lons)
    mixing_grad = call(
        functools.partial(last_sum_kernel, normalizer),
        shaped((basis_count, channels // lats, channels), F32),
        (place, part, swap(part, "z", 8, 1), swap(part, "xl", 2, 1), swap(part, LON, 16, 9)),
        [SMEM] + [VMEM] * 4,
        "last_sum",
        flops=part.size * 4,
        moved=part.size * 16,
    )
    return (output, field_grad, mixing_grad)


def solution(mesh):
    grid = Mesh(mesh.devices.reshape(4, 2, 2, 2, 8), ("y", "xh", "core", "xl", "z"))
    return jax.shard_map(
        local,
        mesh=grid,
        in_specs=(P(LAT, LON, None), P(), P(), P(), P(), P(LAT, LON, None)),
        out_specs=(P(LAT, LON, None), P(LAT, LON, None), P(None, LAT, None)),
        check_vma=False,
    )
```

```python
import functools
import math

import jax
import jax.numpy as jnp
from jax import lax
from jax.experimental import pallas as pl
from jax.experimental.pallas import tpu as pltpu
from jax.sharding import Mesh
from jax.sharding import PartitionSpec as P

HL = 2
MIXED_COST = 60_000_000_000
FILTER_COST = 20_000_000_000
WL = 16
SPAN = 2 * HL + 1
F32 = jnp.float32
BF16 = jnp.bfloat16
VMEM = pl.BlockSpec(memory_space=pltpu.VMEM)
SMEM = pl.BlockSpec(memory_space=pltpu.SMEM)
PARAMS = pltpu.CompilerParams(vmem_limit_bytes=16 * 1024 * 1024)


def iota(shape, axis):
    return lax.broadcasted_iota(jnp.int32, shape, axis)


def placed_lines(weights, distance, count):
    kinds = iota((weights.shape[0], 1), 0) % count
    return jnp.where(distance == kinds, weights, 0.0)


def store_bands(out, row, lines, basis_count, count, taps):
    cols = out.shape[1] // basis_count
    width = out.shape[2]
    for basis in range(basis_count):
        first = basis * count
        line = lines[first : first + 1]
        for tap in range(1, taps):
            line = line + lines[first + tap : first + tap + 1]
        for lane in range(0, width, 128):
            tile = jnp.broadcast_to(line[:, lane : lane + 128], (cols, 128))
            tile = pltpu.roll(tile, 0, 1, stride=1, stride_axis=0).astype(BF16)
            room = min(128, width - lane)
            out[row, basis * cols : (basis + 1) * cols, lane : lane + room] = tile[:, :room]


def gathered(near_all, place, psi, lat, lon, rows):
    basis_count, blocks, taps, cycles = psi.shape
    lines = basis_count * (taps + 2)
    cycle = iota((cycles, 128), 0) - place[0] + HL
    hot = ((iota((cycles, 128), 1) == cycle) & (cycle < rows + 2 * HL)).astype(BF16)
    for block in range(blocks):
        turns = [lon[block : block + 1].astype(F32), lat[block : block + 1].astype(F32)]
        here = []
        for basis in range(basis_count):
            here += [psi[basis, block].astype(F32)] + turns
        here = jnp.concatenate(here, axis=0).astype(BF16)
        near_all[block * lines : (block + 1) * lines] = jnp.dot(
            here, hot, preferred_element_type=F32
        ).astype(BF16)


def forward_taps_kernel(place, psi, lat, lon, forward, near_all, spread):
    rows = forward.shape[0] - 2 * HL
    basis_count, blocks, taps, cycles = psi.shape
    count = taps + 2
    wide = forward.shape[2] // blocks
    lines = basis_count * count
    gathered(near_all, place, psi, lat, lon, rows)
    near = near_all[...]
    slot = iota((128, 128), 0)
    base = iota((1, wide), 1) - WL

    def one_row(row, carry):
        weights_all = jnp.dot(near, (slot == row).astype(BF16), preferred_element_type=F32)
        totals = []
        for block in range(blocks):
            weights = weights_all[block * lines : (block + 1) * lines, :wide]
            distance = base - weights[taps : taps + 1].astype(jnp.int32)
            totals.append(placed_lines(weights, distance, count))
        store_bands(forward, row, jnp.concatenate(totals, axis=1), basis_count, count, taps)
        return carry

    lax.fori_loop(0, rows + 2 * HL, one_row, 0, unroll=20)


def adjoint_taps_kernel(place, after, psi, lat, lon, adjoint, near_all, adj_wide):
    rows = adjoint.shape[0]
    basis_count, blocks, taps, cycles = psi.shape
    count = taps + 2
    wide = adjoint.shape[2] // SPAN
    lines = basis_count * count
    gathered(near_all, place, psi, lat, lon, rows)
    near = near_all[...]
    lanes = adj_wide.shape[1]
    slot = iota((128, lanes), 0) - iota((128, lanes), 1) // wide
    inside = iota((128, lanes), 1) // wide < SPAN
    turn = iota((1, lanes), 1)
    wanted = HL - turn // wide
    base = WL - turn % wide

    def one_row(row, carry):
        adj_wide[...] = jnp.dot(
            near, ((slot == row) & inside).astype(BF16), preferred_element_type=F32
        )
        total = None
        for block in range(blocks):
            weights = adj_wide[block * lines : (block + 1) * lines, :]
            shift = weights[taps : taps + 1].astype(jnp.int32)
            match = weights[taps + 1 : taps + 2].astype(jnp.int32) == wanted
            value = placed_lines(weights, base - jnp.where(match, shift, 4 * wide), count)
            total = value if total is None else total + value
        store_bands(adjoint, row, total, basis_count, count, taps)
        return carry

    lax.fori_loop(0, rows, one_row, 0, unroll=16)


def rims_kernel(place, inner, outer, to_east, to_west):
    cols = inner.shape[2]
    odd = place[3] == 1
    north = jnp.where(odd, inner[...], outer[...])
    south = jnp.where(odd, outer[...], inner[...])
    to_east[0] = north[:, :, cols - WL :]
    to_east[1] = south[:, :, cols - WL :]
    to_west[0] = north[:, :, :WL]
    to_west[1] = south[:, :, :WL]


def assemble(which, place, extended, center, west, east, inner, outer, rims_w, rims_e):
    rows, cols, _ = center.shape
    extended[HL : HL + rows, 0:WL] = west[...]
    extended[HL : HL + rows, WL : WL + cols] = center[...]
    extended[HL : HL + rows, WL + cols :] = east[...]
    odd = place[3] == 1
    above = place[0] > 0
    below = place[0] + rows < place[5]
    none = jnp.zeros((), BF16)
    north = jnp.where(odd, inner[which], outer[which])
    south = jnp.where(odd, outer[which], inner[which])
    for side, (inside, rim, lines) in enumerate(
        ((above, north, slice(0, HL)), (below, south, slice(HL + rows, None)))
    ):
        extended[lines, 0:WL] = jnp.where(inside, rims_w[side, which], none)
        extended[lines, WL : WL + cols] = jnp.where(inside, rim, none)
        extended[lines, WL + cols :] = jnp.where(inside, rims_e[side, which], none)


def terms_kernel(
    place, lat, taps, center, west, east, cot, inner, outer, keep, send, extended, filtered, around
):
    rows, cols, channels = center.shape
    basis_count = filtered.shape[0]
    blocks = lat.shape[0]
    wide_rows = rows + 2 * HL
    extended[0:rows, 0:WL] = west[...]
    extended[0:rows, WL : WL + cols] = center[...]
    extended[0:rows, WL + cols :] = east[...]
    extended[rows] = jnp.zeros(extended.shape[1:], BF16)
    odd = place[3] == 1
    around[0:HL] = jnp.where(odd, inner[1], outer[1])
    around[HL : HL + rows] = cot[...]
    around[HL + rows :] = jnp.where(odd, outer[1], inner[1])

    def one_row(row, carry):
        cycle = jnp.clip(place[0] + row - HL, 0, place[5] - 1)
        slabs = []
        for block in range(blocks):
            source = row - HL + lat[block, cycle]
            inside = (source >= 0) & (source < rows)
            slabs.append(extended[jnp.where(inside, source, rows)])
        slab = jnp.concatenate(slabs, axis=0)
        part = jnp.dot(taps[row], slab, preferred_element_type=F32).astype(BF16)
        filtered[:, row] = part.reshape(basis_count, cols, channels)
        return carry

    lax.fori_loop(0, wide_rows, one_row, 0, unroll=20)
    cot_flat = around[...].reshape(wide_rows * cols, channels)
    pairs = keep.shape[0] // 2
    share = channels // (2 * pairs)
    per = keep.shape[1] // share
    core = place[3]
    for basis in range(basis_count):
        terms = lax.dot_general(
            filtered[basis].reshape(wide_rows * cols, channels),
            cot_flat,
            (((0,), (0,)), ((), ())),
            preferred_element_type=F32,
        ).reshape(pairs, 2, share, channels)
        lines = slice(basis % per * share, (basis % per + 1) * share)
        mine = jnp.where(core == 0, terms[:, 0], terms[:, 1])
        other = jnp.where(core == 0, terms[:, 1], terms[:, 0]).astype(BF16)
        for pair in range(pairs):
            keep[2 * pair + basis // per, lines] = mine[pair]
            send[2 * pair + basis // per, lines] = other[pair]


def ready_kernel(west, east, token):
    token[...] = jnp.zeros_like(token)


def output_kernel(
    place, after, lat, taps, center, west, east, inner, outer, rims_w, rims_e, mixing, out, token, extended, filtered
):
    token[...] = jnp.zeros_like(token)
    rows, cols, channels = center.shape
    basis_count = mixing.shape[0]
    blocks = lat.shape[0]
    assemble(0, place, extended, center, west, east, inner, outer, rims_w, rims_e)

    def one_row(row, carry):
        slabs = [extended[row + HL + lat[block, place[0] + row]] for block in range(blocks)]
        slab = jnp.concatenate(slabs, axis=0)
        part = jnp.dot(taps[row + HL], slab, preferred_element_type=F32).astype(BF16)
        filtered[:, row] = part.reshape(basis_count, cols, channels)
        return carry

    lax.fori_loop(0, rows, one_row, 0, unroll=16)
    total = None
    for basis in range(basis_count):
        part = jnp.dot(
            filtered[basis].reshape(rows * cols, channels),
            mixing[basis],
            preferred_element_type=F32,
        )
        total = part if total is None else total + part
    out[...] = total.reshape(rows, cols, channels).astype(BF16)


def adjoint_kernel(
    place, after, taps, center, west, east, inner, outer, rims_w, rims_e, mixing, out, token, extended, spread
):
    token[...] = jnp.zeros_like(token)
    rows, cols, channels = center.shape
    basis_count = mixing.shape[0]
    assemble(1, place, extended, center, west, east, inner, outer, rims_w, rims_e)

    def one_row(row, carry):
        slab = extended[pl.ds(row, SPAN)].reshape(SPAN * (cols + 2 * WL), channels)
        pulled = jnp.dot(taps[row], slab, preferred_element_type=F32).astype(BF16)
        spread[:, row] = pulled.reshape(basis_count, cols, channels)
        return carry

    lax.fori_loop(0, rows, one_row, 0, unroll=16)
    total = None
    for basis in range(basis_count):
        part = lax.dot_general(
            spread[basis].reshape(rows * cols, channels),
            mixing[basis],
            (((1,), (1,)), ((), ())),
            preferred_element_type=F32,
        )
        total = part if total is None else total + part
    out[...] = total.reshape(rows, cols, channels).astype(BF16)


def pair_sum_kernel(after, keep, recv, out):
    out[...] = (keep[...] + recv[...].astype(F32)).astype(BF16)


def chip_sum_kernel(after_one, after_two, parts, out):
    total = parts[0].astype(F32)
    for chip in range(1, parts.shape[0]):
        total = total + parts[chip].astype(F32)
    out[...] = total.astype(BF16)


def four_sum_kernel(one, two, three, four, out):
    near = one[...].astype(F32) + two[...].astype(F32)
    far = three[...].astype(F32) + four[...].astype(F32)
    out[...] = (near + far).astype(BF16)


def last_sum_kernel(normalizer, place, own, by_z, by_x, by_both, out):
    low = lax.rem(place[2], 2)
    shape = (2,) + out.shape[1:]
    mine = own[...].astype(F32) + by_z[...].astype(F32)
    other = by_x[...].astype(F32) + by_both[...].astype(F32)
    out[pl.ds(2 * low, 2)] = (mine * normalizer).reshape(shape)
    out[pl.ds(2 * (1 - low), 2)] = (other * normalizer).reshape(shape)


LAT = ("y", "xh", "core")
LON = ("xl", "z")
CROSS = ("xh", "xl")


def shift(cells, axis, count, step):
    return lax.ppermute(cells, axis, [(i, (i + step) % count) for i in range(count)])


def swap(cells, axis, count, mask):
    return lax.ppermute(cells, axis, [(i, i ^ mask) for i in range(count)])


def call(kernel, outs, args, specs, name, scratch=(), flops=0, moved=0):
    return pl.pallas_call(
        kernel,
        out_shape=outs,
        in_specs=specs,
        out_specs=jax.tree.map(lambda _: VMEM, outs),
        scratch_shapes=list(scratch),
        compiler_params=PARAMS,
        cost_estimate=pl.CostEstimate(flops=flops, bytes_accessed=moved, transcendentals=0),
        name=name,
    )(*args)


def shaped(shape, dtype):
    return jax.ShapeDtypeStruct(shape, dtype)


def local(field, filter_values, block_lat, block_lon, mixing, cotangent):
    rows, cols, channels = field.shape
    basis_count, _, blocks, taps = filter_values.shape
    lats = lax.axis_size(LAT)
    lons = lax.axis_size(LON)
    place = jnp.stack(
        [
            lax.axis_index(LAT) * rows,
            lax.axis_index("y"),
            lax.axis_index(CROSS),
            lax.axis_index("core"),
            lax.axis_index("z"),
            jnp.int32(rows * lats),
        ]
    ).astype(jnp.int32)
    both = (field, cotangent)
    odd = lax.axis_index("core") == 1
    top = jnp.stack([cells[:HL] for cells in both])
    bottom = jnp.stack([cells[rows - HL :] for cells in both])
    inner = jnp.where(odd, top, bottom)
    outer = jnp.where(odd, bottom, top)
    west = shift(field[:, cols - WL :], LON, lons, 1)
    east = shift(field[:, :WL], LON, lons, -1)
    psi = filter_values.transpose(0, 2, 3, 1)
    lat = block_lat.T
    lon = block_lon.T
    wide = cols + 2 * WL
    lines = basis_count * blocks * (taps + 2)
    fwd_taps = call(
        forward_taps_kernel,
        shaped((rows + 2 * HL, basis_count * cols, blocks * wide), BF16),
        (place, psi, lat, lon),
        [SMEM] + [VMEM] * 3,
        "forward_taps",
        [pltpu.VMEM((lines, 128), BF16), pltpu.VMEM((lines, 128), F32)],
        flops=1_000_000_000,
        moved=1_000_000,
    )
    inner = swap(inner, LAT, lats, 1)
    pairs = [(0, 0), (lats - 1, lats - 1)]
    for low in range(1, lats - 1, 2):
        pairs += [(low, low + 1), (low + 1, low)]
    outer = lax.ppermute(outer, LAT, pairs)
    rim = shaped((2, 2, HL, WL, channels), BF16)
    rim_to_east, rim_to_west = call(
        rims_kernel, (rim, rim), (place, inner, outer), [SMEM] + [VMEM] * 2, "rims", moved=1_000_000
    )
    rims_w = shift(rim_to_east, LON, lons, 1)
    rims_e = shift(rim_to_west, LON, lons, -1)
    share = basis_count * channels // lats
    keep, send = call(
        terms_kernel,
        (
            shaped((lats, share // 2, channels), F32),
            shaped((lats, share // 2, channels), BF16),
        ),
        (place, lat, fwd_taps, field, west, east, cotangent, inner, outer),
        [SMEM] * 2 + [VMEM] * 7,
        "terms",
        [
            pltpu.VMEM((rows + 1, wide, channels), BF16),
            pltpu.VMEM((basis_count, rows + 2 * HL, cols, channels), BF16),
            pltpu.VMEM((rows + 2 * HL, cols, channels), BF16),
        ],
        flops=FILTER_COST,
        moved=8_000_000,
    )
    recv = swap(send, "core", 2, 1)
    cot_west = shift(cotangent[:, cols - WL :], LON, lons, 1)
    cot_east = shift(cotangent[:, :WL], LON, lons, -1)
    token = shaped((8, 128), F32)
    ready = call(
        ready_kernel,
        token,
        (cot_west, cot_east),
        [VMEM] * 2,
        "ready",
        flops=MIXED_COST,
        moved=1_000_000,
    )
    summed = call(
        pair_sum_kernel,
        shaped(keep.shape, BF16),
        (ready, keep, recv),
        [VMEM] * 3,
        "pair_sum",
        flops=keep.size,
        moved=keep.size * 8,
    )
    parts = lax.all_to_all(summed, ("y", "xh", "xl"), 0, 0)

    output, token_one = call(
        output_kernel,
        (shaped((rows, cols, channels), BF16), token),
        (
            place,
            summed,
            lat,
            fwd_taps,
            field,
            west,
            east,
            inner,
            outer,
            rims_w,
            rims_e,
            mixing,
        ),
        [SMEM, VMEM, SMEM] + [VMEM] * 9,
        "output",
        [
            pltpu.VMEM((rows + 2 * HL, wide, channels), BF16),
            pltpu.VMEM((basis_count, rows, cols, channels), BF16),
        ],
        flops=3_000_000_000,
        moved=6_000_000,
    )
    adj_taps = call(
        adjoint_taps_kernel,
        shaped((rows, basis_count * cols, SPAN * wide), BF16),
        (place, summed, psi, lat, lon),
        [SMEM] + [VMEM] * 4,
        "adjoint_taps",
        [
            pltpu.VMEM((lines, 128), BF16),
            pltpu.VMEM((lines, -(-SPAN * wide // 128) * 128), F32),
        ],
        flops=2_000_000_000,
        moved=2_000_000,
    )
    field_grad, token_two = call(
        adjoint_kernel,
        (shaped((rows, cols, channels), BF16), token),
        (
            place,
            summed,
            adj_taps,
            cotangent,
            cot_west,
            cot_east,
            inner,
            outer,
            rims_w,
            rims_e,
            mixing,
        ),
        [SMEM, VMEM] + [VMEM] * 9,
        "adjoint",
        [
            pltpu.VMEM((rows + 2 * HL, wide, channels), BF16),
            pltpu.VMEM((basis_count, rows, cols, channels), BF16),
        ],
        flops=3_000_000_000,
        moved=6_000_000,
    )

    _, deep, _ = parts.shape
    part = call(
        chip_sum_kernel,
        shaped((deep, channels), BF16),
        (token_one, token_two, parts),
        [VMEM] * 3,
        "chip_sum",
        flops=parts.size,
        moved=parts.size * 2,
    )
    part = call(
        four_sum_kernel,
        shaped((deep, channels), BF16),
        (part, *(swap(part, "z", 8, mask) for mask in (2, 4, 6))),
        [VMEM] * 4,
        "four_sum",
        flops=part.size * 4,
        moved=part.size * 10,
    )
    normalizer = 1.0 / math.sqrt(rows * lats * cols * lons)
    mixing_grad = call(
        functools.partial(last_sum_kernel, normalizer),
        shaped((basis_count, channels // lats, channels), F32),
        (place, part, swap(part, "z", 8, 1), swap(part, "xl", 2, 1), swap(part, LON, 16, 9)),
        [SMEM] + [VMEM] * 4,
        "last_sum",
        flops=part.size * 4,
        moved=part.size * 16,
    )
    return (output, field_grad, mixing_grad)


def solution(mesh):
    grid = Mesh(mesh.devices.reshape(4, 2, 2, 2, 8), ("y", "xh", "core", "xl", "z"))
    return jax.shard_map(
        local,
        mesh=grid,
        in_specs=(P(LAT, LON, None), P(), P(), P(), P(), P(LAT, LON, None)),
        out_specs=(P(LAT, LON, None), P(LAT, LON, None), P(None, LAT, None)),
        check_vma=False,
    )
```
